32 devices in a mesh: leaf: 2 (over x), row: 4 (over z), col: 4 (over y, core).
Axes of the slice: x: 2, y: 2, z: 4, core: 2. Of those that a mesh axis runs over, the one named last changes fastest.
Arguments:
- leaf_rhs: float32 [4, 16, 4096], P('leaf', None, 'col'), may hold values from -6 to 6
- leaf_inverse: float32 [4, 4096, 4096], P('leaf', 'row', 'col'), as said below
- update_rows: float32 [4, 2048, 4096], P('leaf', 'col', 'row'), may hold values from -0.09375 to 0.09375
- update_map: int32 [4, 16], P('leaf'), may hold values from 0 to 31, as said below
- sep_rhs: float32 [16, 4096], replicated, may hold values from -6 to 6
- sep_inverse: float32 [4096, 4096], P(('leaf', 'row', 'col')), as said below
Outputs:
- leaf_solution: float32 [4, 16, 4096], P('leaf', None, ('col', 'row'))
- sep_solution: float32 [16, 4096], P(None, ('leaf', 'row', 'col'))
The draws below stay inside these ranges and needn't reach their ends.
Inputs may be any that keep to these rules, and one draw needn't show every extreme that they name: `update_map`: each row names 16 different separator blocks. `leaf_inverse`: entries off the diagonal are independent and of order 1 / sqrt(4096); each diagonal entry is one plus such a term. `sep_inverse`: entries off the diagonal are independent and of order 1 / sqrt(4096); each diagonal entry is one plus such a term.
All inputs are finite; a program needn't handle non-finite values.
Results may differ from the reference program's by a relative error of at most 0.000068.
Values sent between devices are 32-bit elements; how exact they have to be, the bound alone decides.
No kernel may reach another device: no remote copies, remote signals or barrier semaphores. Data moves between devices by JAX's collectives and lax.ppermute only.
A program may use at most 64 MiB of HBM per device.

```python
import jax
import jax.numpy as jnp
from jax import lax

NL = 4096
NS = 4096
NRHS = 16
BLOCK = 128
NBLK = 16
SUBTREES = 4
NUP = 2048


def near_identity(key, count, order):
    noise = jax.random.normal(jax.random.fold_in(key, 11), (count, order, order), jnp.float32)
    return jnp.eye(order, dtype=jnp.float32)[None] + 0.7 * noise / jnp.sqrt(jnp.float32(order))


def draw_leaf_inverse(key, part):
    return near_identity(key, SUBTREES, NL)


def draw_sep_inverse(key, part):
    return near_identity(jax.random.fold_in(key, 5), 1, NS)[0]


def draw_update_map(key, part):
    keys = jax.random.split(jax.random.fold_in(key, 7), SUBTREES)
    picks = jax.vmap(lambda k: jax.random.permutation(k, NS // BLOCK)[:NBLK])(keys)
    return picks.astype(jnp.int32)


def block_levels(own_key, dims, cuts, low, largest):
    level = 1.0
    for position, shards_of in cuts:
        steps = jax.random.uniform(jax.random.fold_in(jax.random.fold_in(own_key, 6), position), (shards_of,), jnp.float32, low / len(cuts), largest / len(cuts))
        level = level * jnp.repeat(jnp.exp(steps), dims[position] // shards_of).reshape((-1,) + (1,) * (len(dims) - 1 - position))
    return level


def scatter_about(stream_key, dims, width, limit, shards=(), held_as=jnp.bfloat16):
    result = jax.random.normal(stream_key, dims, jnp.float32) * width
    if len(shards) > 0:
        result = block_levels(stream_key, dims, shards, -0.22, 0.18) * result
    return jnp.clip(result, min=-limit, max=limit).astype(held_as)


def setup_inputs(seed: int = 0) -> dict:
    splits = jax.random.split(jax.random.key(seed), 7)
    leaf_rhs = scatter_about(splits[0], (SUBTREES, NRHS, NL), 1.0, 6.0, ((0, 2), (2, 4)), jnp.float32)
    leaf_inverse = draw_leaf_inverse(jax.random.fold_in(splits[6], 71), 0)
    update_rows = scatter_about(splits[2], (SUBTREES, NUP, NL), NL ** -0.5, 0.09375, ((0, 2), (1, 4), (2, 4)), jnp.float32)
    update_map = draw_update_map(jax.random.fold_in(splits[6], 71), 0)
    sep_rhs = scatter_about(splits[4], (NRHS, NS), 1.0, 6.0, (), jnp.float32)
    sep_inverse = draw_sep_inverse(jax.random.fold_in(splits[6], 71), 0)
    return dict(leaf_rhs=leaf_rhs, leaf_inverse=leaf_inverse, update_rows=update_rows, update_map=update_map, sep_rhs=sep_rhs, sep_inverse=sep_inverse)


HIGH = lax.Precision.HIGHEST


def reference(leaf_rhs, leaf_inverse, update_rows, update_map, sep_rhs, sep_inverse):
    nsb = NS // BLOCK
    subs = leaf_rhs.shape[0]
    forward = jnp.einsum('sij,srj->sri', leaf_inverse, leaf_rhs, precision=HIGH)
    coupled = jnp.einsum('sun,srn->sru', update_rows, forward, precision=HIGH)
    onehot = (update_map[:, :, None] == jnp.arange(nsb, dtype=jnp.int32)[None, None, :]).astype(jnp.float32)
    blocks = coupled.reshape(subs, NRHS, NBLK, BLOCK)
    scattered = jnp.einsum('srkc,skb->rbc', blocks, onehot, precision=HIGH).reshape(NRHS, NS)
    sep_forward = jnp.einsum('ij,rj->ri', sep_inverse, sep_rhs - scattered, precision=HIGH)
    sep_solution = jnp.einsum('ij,ri->rj', sep_inverse, sep_forward, precision=HIGH)
    pulled = jnp.einsum('rbc,skb->srkc', sep_solution.reshape(NRHS, nsb, BLOCK), onehot, precision=HIGH)
    pulled = pulled.reshape(subs, NRHS, NBLK * BLOCK)
    reduced = forward - jnp.einsum('sun,sru->srn', update_rows, pulled, precision=HIGH)
    leaf_solution = jnp.einsum('sij,sri->srj', leaf_inverse, reduced, precision=HIGH)
    return leaf_solution, sep_solution
```

```python
import functools

import jax
import jax.numpy as jnp
from jax import lax
from jax.sharding import PartitionSpec as P

BLOCK = 128
CORES = 2

HIGH = lax.Precision.HIGHEST


def swap(value, axes, size, mask):
    return lax.ppermute(value, axes, [(i, i ^ mask) for i in range(size)])


def picked(value, dim, index, count):
    return jnp.stack(
        [lax.dynamic_index_in_dim(value, index ^ m, dim, keepdims=False) for m in range(count)], dim
    )


def halves(value, core):
    half = value.shape[0] // CORES
    mine = lax.dynamic_slice_in_dim(value, core * half, half, 0)
    other = lax.dynamic_slice_in_dim(value, (1 - core) * half, half, 0)
    return mine, other


def sum_over_col(terms, cols, core):
    mine, other = halves(terms, core)
    mine = mine + swap(other, "col", cols, 1)
    step = CORES
    while step < cols:
        mine = mine + swap(mine, "col", cols, step)
        step *= 2
    other = swap(mine, "col", cols, 1)
    return jnp.where(
        core == 0, jnp.concatenate([mine, other]), jnp.concatenate([other, mine])
    )


def body(sizes, leaf_rhs, leaf_inverse, update_rows, update_map, sep_rhs, sep_inverse):
    leaves, rows, cols = sizes
    chips = leaves * cols // CORES
    subs, nrhs, _ = leaf_rhs.shape
    width = sep_rhs.shape[1]
    blocks_total = width // BLOCK
    blocks_here = update_rows.shape[1] // BLOCK
    sep_rows = sep_inverse.shape[0]
    leaf, row, col = (lax.axis_index(a) for a in ("leaf", "row", "col"))
    core = col % CORES
    plane = leaf * (cols // CORES) + col // CORES

    maps = lax.all_gather(update_map, "leaf")
    maps = maps.reshape(leaves, subs, cols // CORES, CORES, blocks_here)
    maps = maps.transpose(0, 2, 3, 1, 4).reshape(chips, CORES, subs, blocks_here)
    onehot = (maps[..., None] == jnp.arange(blocks_total, dtype=jnp.int32)).astype(jnp.float32)

    partial_fwd = jnp.einsum("sij,srj->sri", leaf_inverse, leaf_rhs, precision=HIGH)
    forward = sum_over_col(partial_fwd, cols, core)
    coupled = jnp.einsum("sun,srn->sru", update_rows, forward, precision=HIGH)
    coupled = coupled + sum(swap(coupled, "row", rows, k) for k in range(1, rows))
    plane_axes, plane_size = ("leaf", "col"), leaves * cols
    pieces = jnp.stack(
        [coupled] + [swap(coupled, plane_axes, plane_size, CORES * m) for m in range(1, chips)]
    )
    others = swap(pieces, "col", cols, 1)
    pieces = jnp.stack([pieces, others], 1).reshape(
        chips, CORES, subs, nrhs, blocks_here, BLOCK
    )
    spread = picked(picked(onehot, 0, plane, chips), 1, core, CORES)
    contrib = jnp.einsum("pqsrkc,pqskb->rbc", pieces, spread, precision=HIGH)
    updated = sep_rhs - contrib.reshape(nrhs, width)

    sep_forward = jnp.einsum("ij,rj->ri", sep_inverse, updated, precision=HIGH)
    back_terms = jnp.einsum("ij,ri->rj", sep_inverse, sep_forward, precision=HIGH)
    pulls = jnp.einsum(
        "rbc,pqskb->qpsrkc",
        back_terms.reshape(nrhs, blocks_total, BLOCK),
        spread,
        precision=HIGH,
    ).reshape(CORES, chips, subs, nrhs, blocks_here * BLOCK)
    own = back_terms.reshape(nrhs, leaves, rows, cols // CORES, CORES, sep_rows)
    own = own.transpose(4, 1, 3, 0, 2, 5).reshape(CORES, chips, nrhs, rows, sep_rows)
    own = picked(picked(own, 0, core, CORES), 1, plane, chips)
    pulls = pulls[0] + swap(pulls[1], "col", cols, 1)
    own = own[0] + swap(own[1], "col", cols, 1)
    pulled = pulls[0] + sum(
        swap(pulls[m], plane_axes, plane_size, CORES * m) for m in range(1, chips)
    )
    own = own[0] + sum(swap(own[m], plane_axes, plane_size, CORES * m) for m in range(1, chips))
    pulled = pulled + sum(swap(pulled, "row", rows, k) for k in range(1, rows))
    own = picked(own, 1, row, rows)
    sep_solution = own[:, 0] + sum(swap(own[:, k], "row", rows, k) for k in range(1, rows))

    pull_terms = jnp.einsum("sun,sru->srn", update_rows, pulled, precision=HIGH)
    reduced = forward - sum_over_col(pull_terms, cols, core)
    terms = jnp.einsum("sij,sri->srj", leaf_inverse, reduced, precision=HIGH)
    terms = picked(terms.reshape(subs, nrhs, rows, -1), 2, row, rows)
    leaf_solution = terms[:, :, 0] + sum(
        swap(terms[:, :, k], "row", rows, k) for k in range(1, rows)
    )
    return (leaf_solution, sep_solution)


def solution(mesh):
    sizes = tuple(mesh.shape[a] for a in ("leaf", "row", "col"))
    in_specs = (
        P("leaf", None, "col"),
        P("leaf", "row", "col"),
        P("leaf", "col", "row"),
        P("leaf", None),
        P(),
        P(("leaf", "row", "col"), None),
    )
    out_specs = (P("leaf", None, ("col", "row")), P(None, ("leaf", "row", "col")))
    return jax.shard_map(
        functools.partial(body, sizes), mesh=mesh, in_specs=in_specs, out_specs=out_specs, check_vma=False
    )
```

```python
import functools

import jax
import jax.numpy as jnp
from jax import lax
from jax.experimental import pallas as pl
from jax.experimental.pallas import tpu as pltpu
from jax.sharding import PartitionSpec as P

BLOCK = 128
CORES = 2
MIB = 1 << 20

F32, BF16 = jnp.float32, jnp.bfloat16
HBM = pl.BlockSpec(memory_space=pltpu.HBM)
SCALARS = pl.BlockSpec(memory_space=pltpu.SMEM)
WHOLE = pl.BlockSpec(memory_space=pltpu.VMEM)


def in_hbm(value):
    return pltpu.with_memory_space_constraint(value, pltpu.HBM)


def split(value):
    high = value.astype(BF16)
    return high, (value - high.astype(F32)).astype(BF16)


def dot3(value, matrix, dims):
    rows = value.shape[0]
    high, low = split(matrix)
    parts = jnp.concatenate(split(value))
    main = lax.dot_general(parts, high, dims, preferred_element_type=F32)
    rest = lax.dot_general(parts[:rows], low, dims, preferred_element_type=F32)
    return main[:rows] + (main[rows:] + rest)


ROWS_OF = (((1,), (1,)), ((), ()))
COLUMNS_OF = (((1,), (0,)), ((), ()))


def sub_of(slot, half, core):
    return core * half + slot if slot < half else (1 - core) * half + (slot - half)


def chunk_of(rows):
    return min(rows, 512)


def leaf_kernel(rhs, inverse, out, held, land, sems, rhs_sem):
    subs, rows, _ = inverse.shape
    chunk = chunk_of(rows)
    steps = rows // chunk

    def fetch(sub, step):
        part = pl.ds(step * chunk, chunk)
        return pltpu.make_async_copy(
            inverse.at[sub, part], land.at[sub, part], sems.at[sub * steps + step]
        )

    first = pltpu.make_async_copy(rhs, held, rhs_sem)
    first.start()
    for sub in range(subs):
        for step in range(steps):
            fetch(sub, step).start()
    first.wait()
    for sub in range(subs):
        for step in range(steps):
            part = pl.ds(step * chunk, chunk)
            fetch(sub, step).wait()
            out[sub, :, part] = dot3(held[sub], land[sub, part], ROWS_OF)


def couple_kernel(place, mine, other, update, out):
    half, up = mine.shape[0], update.shape[1]
    for slot in range(2 * half):
        value = mine[slot] if slot < half else other[slot - half]
        sub = sub_of(slot, half, place[0])
        out[:, slot * up : (slot + 1) * up] = dot3(value, update[sub], ROWS_OF)


def spots(sizes, half, place, maps, chips, side, here):
    lines = sizes[3]
    core = place[0] if side == 0 else 1 - place[0]
    for chip in range(chips):
        first = ((place[2] ^ (chip % lines)) * CORES + core) * here
        for slot in range(2 * half):
            sub = sub_of(slot, half, core)
            for k in range(here):
                at = (slot * here + k) * BLOCK
                yield chip, slice(at, at + BLOCK), maps[chip // lines, sub, first + k]


def scatter_kernel(sizes, half, place, maps, near, rhs, out):
    here = near.shape[2] // (2 * half * BLOCK)
    for b in range(out.shape[0]):
        out[b] = rhs[:, b * BLOCK : (b + 1) * BLOCK]
    for chip, lanes, block in spots(sizes, half, place, maps, near.shape[0], 0, here):
        out[block] -= near[chip, :, lanes]


def separator_kernel(sizes, half, inside, place, maps, far, start, sep, keep, send, *rest):
    _, rows, cols, lines = sizes
    held = rest[-1]
    core, plane = place[0], place[1]
    chips = far.shape[0]
    total = held.shape[0]
    here = far.shape[2] // (2 * half * BLOCK)

    held[...] = start[...]
    for chip, lanes, block in spots(sizes, half, place, maps, chips, 1, here):
        held[block] -= far[chip, :, lanes]
    updated = jnp.concatenate([held[b] for b in range(total)], 1)
    forward = dot3(updated, sep[...], ROWS_OF)
    terms = dot3(forward, sep[...], COLUMNS_OF)
    for b in range(total):
        held[b] = terms[:, b * BLOCK : (b + 1) * BLOCK]
    for side, out in ((1, send), (0, keep)):
        for chip, lanes, block in spots(sizes, half, place, maps, chips, side, here):
            out[chip, :, lanes] = held[block]
    if not inside:
        rest[0][...] = terms
        return
    wide = sep.shape[0] // BLOCK
    for side, out in ((1, send), (0, keep)):
        for chip in range(chips):
            other = plane ^ chip
            col = (other % lines) * CORES + (core if side == 0 else 1 - core)
            for row in range(rows):
                for w in range(wide):
                    block = ((other // lines * rows + row) * cols + col) * wide + w
                    at = (2 * half * here + row * wide + w) * BLOCK
                    out[chip, :, at : at + BLOCK] = held[block]


def pull_kernel(place, pulled, update, mine, other):
    half, up = mine.shape[0], update.shape[1]
    for slot in [*range(half, 2 * half), *range(half)]:
        out, at = (mine, slot) if slot < half else (other, slot - half)
        value = pulled[:, slot * up : (slot + 1) * up]
        out[at] = dot3(value, update[sub_of(slot, half, place[0])], COLUMNS_OF)


def solve_kernel(place, mine, other, pull_mine, pull_other, inverse, out):
    half = mine.shape[0]
    for slot in range(2 * half):
        if slot < half:
            value = mine[slot] - pull_mine[slot]
        else:
            value = other[slot - half] - pull_other[slot - half]
        sub = sub_of(slot, half, place[0])
        out[sub] = dot3(value, inverse[sub], COLUMNS_OF)


def finish_kernel(*refs):
    *parts, leaf_out, sep_out = refs
    share = leaf_out.shape[2]
    done = sum(part[...] for part in parts[1:]) + parts[0][...]
    for sub in range(leaf_out.shape[0]):
        leaf_out[sub] = done[:, sub * share : (sub + 1) * share]
    sep_out[...] = done[:, leaf_out.shape[0] * share :]


def swap(value, axes, size, mask):
    return lax.ppermute(value, axes, [(i, i ^ mask) for i in range(size)])


def picked(value, dim, index, count):
    return jnp.stack(
        [lax.dynamic_index_in_dim(value, index ^ m, dim, keepdims=False) for m in range(count)], dim
    )


def halves(value, core):
    half = value.shape[0] // CORES
    return tuple(lax.dynamic_slice_in_dim(value, c * half, half, 0) for c in (core, 1 - core))


def sum_over_lines(mine, cols):
    step = CORES
    while step < cols:
        mine = mine + swap(mine, "col", cols, step)
        step *= 2
    return mine, swap(mine, "col", cols, 1)


def call(kernel, out_shape, in_specs, limit, cost, scratch=()):
    flops, nbytes = cost
    return pl.pallas_call(
        kernel,
        out_shape=out_shape,
        in_specs=in_specs,
        scratch_shapes=scratch,
        compiler_params=pltpu.CompilerParams(vmem_limit_bytes=limit * MIB),
        cost_estimate=pl.CostEstimate(flops=flops, bytes_accessed=nbytes, transcendentals=0),
    )


def body(sizes, leaf_rhs, leaf_inverse, update_rows, update_map, sep_rhs, sep_inverse):
    leaves, rows, cols = sizes
    lines = cols // CORES
    chips = leaves * lines
    subs, nrhs, _ = leaf_rhs.shape
    half = subs // CORES
    width = sep_rhs.shape[1]
    sep_rows = sep_inverse.shape[0]
    _, leaf_rows, leaf_cols = leaf_inverse.shape
    up = update_rows.shape[1]
    leaf, row, col = (lax.axis_index(a) for a in ("leaf", "row", "col"))
    core, line = col % CORES, col // CORES
    plane = leaf * lines + line
    place = jnp.stack([core, plane, line]).astype(jnp.int32)
    plane_axes, plane_size = ("leaf", "col"), leaves * cols

    vec = jax.ShapeDtypeStruct((half, nrhs, leaf_rows), F32)
    leaf_flops = 2 * nrhs * leaf_inverse.size
    forward = call(
        leaf_kernel,
        jax.ShapeDtypeStruct((subs, nrhs, leaf_rows), F32),
        [HBM, HBM],
        24,
        (leaf_flops, 4 * leaf_inverse.size),
        (
            pltpu.VMEM(leaf_rhs.shape, F32),
            pltpu.VMEM(leaf_inverse.shape, F32),
            pltpu.SemaphoreType.DMA((subs * (leaf_rows // chunk_of(leaf_rows)),)),
            pltpu.SemaphoreType.DMA,
        ),
    )(in_hbm(leaf_rhs), in_hbm(leaf_inverse))
    forward, leaf_inverse, update_rows, sep_inverse, sep_rhs = lax.optimization_barrier(
        (forward, leaf_inverse, update_rows, sep_inverse, sep_rhs)
    )
    mine, other = halves(forward, core)
    mine = mine + swap(other, "col", cols, 1)
    mine, update_map = lax.optimization_barrier((mine, update_map))
    maps = [update_map] + [swap(update_map, "leaf", leaves, m) for m in range(1, leaves)]
    mine, other = sum_over_lines(mine, cols)
    mine, other, maps = lax.optimization_barrier((mine, other, maps))
    maps = jnp.stack(maps)
    update_cost = (2 * nrhs * update_rows.size, 4 * update_rows.size)
    coupled = call(
        couple_kernel,
        jax.ShapeDtypeStruct((nrhs, subs * up), F32),
        [SCALARS] + [WHOLE] * 3,
        12,
        update_cost,
    )(place, mine, other, update_rows)
    coupled = coupled + sum(swap(coupled, "row", rows, k) for k in range(1, rows))
    near = jnp.stack(
        [coupled] + [swap(coupled, plane_axes, plane_size, CORES * m) for m in range(1, chips)]
    )
    far = swap(near, "col", cols, 1)

    shape = (leaves, rows, cols, lines)
    start = call(
        functools.partial(scatter_kernel, shape, half),
        jax.ShapeDtypeStruct((width // BLOCK, nrhs, BLOCK), F32),
        [SCALARS, SCALARS, WHOLE, WHOLE],
        4,
        (2 * nrhs * width, 12 * nrhs * width),
    )(place, maps, near, sep_rhs)
    inside = sep_rows % BLOCK == 0
    own_width = rows * sep_rows
    length = subs * up + (own_width if inside else 0)
    piece = jax.ShapeDtypeStruct((chips, nrhs, length), F32)
    keep, send, *back = call(
        functools.partial(separator_kernel, shape, half, inside),
        (piece, piece) + (() if inside else (jax.ShapeDtypeStruct((nrhs, width), F32),)),
        [SCALARS, SCALARS] + [WHOLE] * 3,
        12,
        (4 * nrhs * sep_inverse.size, 4 * sep_inverse.size),
        (pltpu.VMEM((width // BLOCK, nrhs, BLOCK), F32),),
    )(place, maps, far, start, sep_inverse)
    if not inside:
        own = back[0].reshape(nrhs, leaves, rows, lines, CORES, sep_rows)
        own = own.transpose(4, 1, 3, 0, 2, 5).reshape(CORES, chips, nrhs, own_width)
        own = picked(picked(own, 0, core, CORES), 1, plane, chips)
        keep = jnp.concatenate([keep, own[0]], 2)
        send = jnp.concatenate([send, own[1]], 2)
    keep = keep + swap(send, "col", cols, 1)
    pulled = keep[0] + sum(swap(keep[m], plane_axes, plane_size, CORES * m) for m in range(1, chips))
    own = pulled[:, subs * up :].reshape(nrhs, rows, sep_rows)
    pulled = pulled[:, : subs * up]
    pulled = pulled + sum(swap(pulled, "row", rows, k) for k in range(1, rows))

    pull_mine, pull_other = call(
        pull_kernel, (vec, vec), [SCALARS, WHOLE, WHOLE], 12, update_cost
    )(place, pulled, update_rows)
    pull_mine = pull_mine + swap(pull_other, "col", cols, 1)
    pull_mine, pull_other = sum_over_lines(pull_mine, cols)
    terms = call(
        solve_kernel,
        jax.ShapeDtypeStruct((subs, nrhs, leaf_cols), F32),
        [SCALARS] + [WHOLE] * 5,
        16,
        (leaf_flops, 4 * leaf_inverse.size),
    )(place, mine, other, pull_mine, pull_other, leaf_inverse)

    share = leaf_cols // rows

    def last(k):
        at = row ^ k
        leaf_part = lax.dynamic_slice_in_dim(terms, at * share, share, 2)
        own_part = lax.dynamic_index_in_dim(own, at, 1, keepdims=False)
        return jnp.concatenate([*leaf_part, own_part], 1)

    parts = [last(0)] + [swap(last(k), "row", rows, k) for k in range(1, rows)]
    if inside and share % BLOCK == 0:
        return call(
            finish_kernel,
            (
                jax.ShapeDtypeStruct((subs, nrhs, share), F32),
                jax.ShapeDtypeStruct((nrhs, sep_rows), F32),
            ),
            [WHOLE] * rows,
            4,
            (parts[0].size * rows, 4 * parts[0].size * rows),
        )(*parts)
    done = sum(parts[1:]) + parts[0]
    leaf_solution = jnp.stack([done[:, s * share : (s + 1) * share] for s in range(subs)])
    return (leaf_solution, done[:, subs * share :])


def solution(mesh):
    sizes = tuple(mesh.shape[a] for a in ("leaf", "row", "col"))
    in_specs = (
        P("leaf", None, "col"),
        P("leaf", "row", "col"),
        P("leaf", "col", "row"),
        P("leaf", None),
        P(),
        P(("leaf", "row", "col"), None),
    )
    out_specs = (P("leaf", None, ("col", "row")), P(None, ("leaf", "row", "col")))
    return jax.shard_map(
        functools.partial(body, sizes), mesh=mesh, in_specs=in_specs, out_specs=out_specs, check_vma=False
    )
```

```python
import functools

import jax
import jax.numpy as jnp
from jax import lax
from jax.experimental import pallas as pl
from jax.experimental.pallas import tpu as pltpu
from jax.sharding import PartitionSpec as P

BLOCK = 128
CORES = 2
MIB = 1 << 20

F32, BF16 = jnp.float32, jnp.bfloat16
HBM = pl.BlockSpec(memory_space=pltpu.HBM)
WHOLE = pl.BlockSpec(memory_space=pltpu.VMEM)


def in_hbm(value):
    return pltpu.with_memory_space_constraint(value, pltpu.HBM)


def in_vmem(value):
    return pltpu.with_memory_space_constraint(value, pltpu.VMEM)


def split(value):
    high = value.astype(BF16)
    return high, (value - high.astype(F32)).astype(BF16)


def dot3(value, halves, dims):
    rows = value.shape[0]
    high, low = halves
    parts = jnp.concatenate(split(value))
    main = lax.dot_general(parts, high, dims, preferred_element_type=F32)
    rest = lax.dot_general(parts[:rows], low, dims, preferred_element_type=F32)
    return main[:rows] + (main[rows:] + rest)


ROWS_OF = (((1,), (1,)), ((), ()))
COLUMNS_OF = (((1,), (0,)), ((), ()))


def sub_of(slot, half, core):
    return core * half + slot if slot < half else (1 - core) * half + (slot - half)


def chunk_of(rows):
    return min(rows, 512)


def leaf_kernel(rhs, inverse, mine, other, held, land, sems, rhs_sem):
    subs, rows, _ = inverse.shape
    half = subs // CORES
    core = lax.axis_index("col") % CORES
    chunk = chunk_of(rows)
    steps = rows // chunk
    order = [*range(half, subs), *range(half)]

    def fetch(slot, step):
        part = pl.ds(step * chunk, chunk)
        return pltpu.make_async_copy(
            inverse.at[sub_of(slot, half, core), part], land.at[slot, part], sems.at[slot * steps + step]
        )

    first = pltpu.make_async_copy(rhs, held, rhs_sem)
    first.start()
    for slot in order:
        for step in range(steps):
            fetch(slot, step).start()
    first.wait()
    for slot in order:
        out, at = (mine, slot) if slot < half else (other, slot - half)
        value = held[sub_of(slot, half, core)]
        for step in range(steps):
            part = pl.ds(step * chunk, chunk)
            fetch(slot, step).wait()
            out[at, :, part] = dot3(value, split(land[slot, part]), ROWS_OF)


def couple_kernel(first, vectors, update, out):
    subs, up, _ = update.shape
    core = lax.axis_index("col") % CORES
    for i in range(vectors.shape[0]):
        matrix = update[sub_of(first + i, subs // CORES, core)]
        out[:, i * up : (i + 1) * up] = dot3(vectors[i], split(matrix), ROWS_OF)


def load_kernel(value, out, sems):
    count = sems.shape[0]
    step = value.shape[0] // count
    copies = [
        pltpu.make_async_copy(
            value.at[pl.ds(i * step, step)], out.at[pl.ds(i * step, step)], sems.at[i]
        )
        for i in range(count)
    ]
    for copy in copies:
        copy.start()
    for copy in copies:
        copy.wait()


def numbers_of(pieces, numbers, sems):
    _, subs, _ = numbers.shape
    at = pieces.shape[2] - BLOCK
    return [
        pltpu.make_async_copy(
            pieces.at[chip, pl.ds(0, subs), pl.ds(at, BLOCK)], numbers.at[chip], sems.at[chip]
        )
        for chip in range(pieces.shape[0])
    ]


def spots(lines, side, numbers, length):
    chips, subs, _ = numbers.shape
    here = length // (subs * BLOCK)
    col = lax.axis_index("col")
    core = (col + side) % CORES
    for chip in range(chips):
        first = ((col // CORES ^ (chip % lines)) * CORES + core) * here
        for slot in range(subs):
            sub = sub_of(slot, subs // CORES, core)
            for k in range(here):
                at = (slot * here + k) * BLOCK
                block = numbers[chip, sub, first + k].astype(jnp.int32)
                yield chip, slice(at, at + BLOCK), block


def scatter_kernel(lines, near, rhs, out, numbers, sems):
    copies = numbers_of(near, numbers, sems)
    for copy in copies:
        copy.start()
    for b in range(out.shape[0]):
        out[b] = rhs[:, b * BLOCK : (b + 1) * BLOCK]
    for copy in copies:
        copy.wait()
    for chip, lanes, block in spots(lines, 0, numbers, near.shape[2] - BLOCK):
        out[block] -= near[chip, :, lanes]


def separator_kernel(sizes, inside, near, far, start, sep, keep, send, *rest):
    leaves, rows, cols, lines = sizes
    *back, held, high, low, ours, theirs, our_sems, their_sems = rest
    chips = far.shape[0]
    total = held.shape[0]
    length = far.shape[2] - BLOCK

    copies = numbers_of(far, theirs, their_sems) + numbers_of(near, ours, our_sems)
    for copy in copies:
        copy.start()
    held[...] = start[...]
    high[...], low[...] = split(sep[...])
    for copy in copies:
        copy.wait()
    for chip, lanes, block in spots(lines, 1, theirs, length):
        held[block] -= far[chip, :, lanes]
    updated = jnp.concatenate([held[b] for b in range(total)], 1)
    forward = dot3(updated, (high[...], low[...]), ROWS_OF)
    terms = dot3(forward, (high[...], low[...]), COLUMNS_OF)
    for b in range(total):
        held[b] = terms[:, b * BLOCK : (b + 1) * BLOCK]
    for side, numbers, out in ((1, theirs, send), (0, ours, keep)):
        for chip, lanes, block in spots(lines, side, numbers, length):
            out[chip, :, lanes] = held[block]
    if not inside:
        back[0][...] = terms
        return
    wide = sep.shape[0] // BLOCK
    me = lax.axis_index("col")
    plane = lax.axis_index("leaf") * lines + me // CORES
    for side, out in ((1, send), (0, keep)):
        for chip in range(chips):
            other = plane ^ chip
            col = (other % lines) * CORES + (me + side) % CORES
            for row in range(rows):
                for w in range(wide):
                    block = ((other // lines * rows + row) * cols + col) * wide + w
                    at = length + (row * wide + w) * BLOCK
                    out[chip, :, at : at + BLOCK] = held[block]


def pull_kernel(first, pulled, update, out):
    subs, up, _ = update.shape
    core = lax.axis_index("col") % CORES
    for i in range(out.shape[0]):
        slot = first + i
        value = pulled[:, slot * up : (slot + 1) * up]
        matrix = update[sub_of(slot, subs // CORES, core)]
        out[i] = dot3(value, split(matrix), COLUMNS_OF)


def reduced_of(mine, other, pull_mine, pull_other):
    half = mine.shape[0]
    core = lax.axis_index("col") % CORES
    for slot in range(2 * half):
        if slot < half:
            value = mine[slot] - pull_mine[slot]
        else:
            value = other[slot - half] - pull_other[slot - half]
        yield slot, sub_of(slot, half, core), value


def solve_kernel(mine, other, pull_mine, pull_other, inverse, out):
    for _, sub, value in reduced_of(mine, other, pull_mine, pull_other):
        out[sub] = dot3(value, split(inverse[sub]), COLUMNS_OF)


def solve_parts_kernel(rows, masks, mine, other, pull_mine, pull_other, own, inverse, *outs):
    subs, _, width = inverse.shape
    share = width // rows
    sep_rows = own.shape[1] // rows
    row = lax.axis_index("row")
    for slot, sub, value in reduced_of(mine, other, pull_mine, pull_other):
        for mask, out in zip(masks, outs, strict=True):
            columns = pl.ds(pl.multiple_of((row ^ mask) * share, share), share)
            terms = dot3(value, split(inverse[sub, :, columns]), COLUMNS_OF)
            out[:, slot * share : (slot + 1) * share] = terms
    for mask, out in zip(masks, outs, strict=True):
        columns = pl.ds(pl.multiple_of((row ^ mask) * sep_rows, sep_rows), sep_rows)
        out[:, subs * share :] = own[:, columns]


def finish_kernel(*refs):
    *parts, leaf_out, sep_out = refs
    subs, _, share = leaf_out.shape
    core = lax.axis_index("col") % CORES
    done = parts[0][...]
    for part in parts[1:]:
        done = done + part[...]
    for slot in range(subs):
        leaf_out[sub_of(slot, subs // CORES, core)] = done[:, slot * share : (slot + 1) * share]
    sep_out[...] = done[:, subs * share :]


def swap(value, axes, size, mask):
    return lax.ppermute(value, axes, [(i, i ^ mask) for i in range(size)])


def picked(value, dim, index, count):
    return jnp.stack(
        [lax.dynamic_index_in_dim(value, index ^ m, dim, keepdims=False) for m in range(count)], dim
    )


def beside(arrived, value):
    value = pl.pallas_call(
        load_kernel,
        out_shape=pltpu.VMEM(value.shape, value.dtype),
        in_specs=[HBM],
        out_specs=pl.BlockSpec(memory_space=pl.ANY),
        scratch_shapes=[pltpu.SemaphoreType.DMA((value.shape[0],))],
        compiler_params=pltpu.CompilerParams(vmem_limit_bytes=MIB),
        cost_estimate=pl.CostEstimate(flops=0, bytes_accessed=4 * value.size, transcendentals=0),
    )(in_hbm(value))
    return lax.optimization_barrier((arrived, value))


def sum_over_lines(mine, cols, arrived=None):
    step = CORES
    while step < cols:
        first = arrived is not None and step == CORES
        mine = mine + (arrived if first else swap(mine, "col", cols, step))
        step *= 2
    return mine, swap(mine, "col", cols, 1)


def call(kernel, out_shape, in_specs, limit, cost, scratch=()):
    flops, nbytes = cost
    return pl.pallas_call(
        kernel,
        out_shape=out_shape,
        in_specs=in_specs,
        scratch_shapes=scratch,
        compiler_params=pltpu.CompilerParams(vmem_limit_bytes=limit * MIB),
        cost_estimate=pl.CostEstimate(flops=flops, bytes_accessed=nbytes, transcendentals=0),
    )


def body(sizes, leaf_rhs, leaf_inverse, update_rows, update_map, sep_rhs, sep_inverse):
    leaves, rows, cols = sizes
    lines = cols // CORES
    chips = leaves * lines
    subs, nrhs, _ = leaf_rhs.shape
    half = subs // CORES
    width = sep_rhs.shape[1]
    sep_rows = sep_inverse.shape[0]
    _, leaf_rows, leaf_cols = leaf_inverse.shape
    up = update_rows.shape[1]
    leaf, row, col = (lax.axis_index(a) for a in ("leaf", "row", "col"))
    core, line = col % CORES, col // CORES
    plane = leaf * lines + line
    plane_axes, plane_size = ("leaf", "col"), leaves * cols

    vec = jax.ShapeDtypeStruct((half, nrhs, leaf_rows), F32)
    leaf_flops = 2 * nrhs * leaf_inverse.size
    mine, other = call(
        leaf_kernel,
        (pltpu.VMEM(vec.shape, F32), pltpu.VMEM(vec.shape, F32)),
        [HBM, HBM],
        61,
        (leaf_flops, 4 * leaf_inverse.size),
        (
            pltpu.VMEM(leaf_rhs.shape, F32),
            pltpu.VMEM(leaf_inverse.shape, F32),
            pltpu.SemaphoreType.DMA((subs * (leaf_rows // chunk_of(leaf_rows)),)),
            pltpu.SemaphoreType.DMA,
        ),
    )(in_hbm(leaf_rhs), in_hbm(leaf_inverse))

    mine = mine + swap(other, "col", cols, 1)
    arrived, update = beside(swap(mine, "col", cols, CORES), update_rows)
    mine, other = sum_over_lines(mine, cols, arrived)
    coupled = [
        call(
            functools.partial(couple_kernel, first),
            jax.ShapeDtypeStruct((nrhs, half * up), F32),
            [WHOLE, WHOLE],
            12,
            (nrhs * update_rows.size, 2 * update_rows.size),
        )(vectors, in_vmem(update))
        for first, vectors in ((0, mine), (half, other))
    ]
    coupled = jnp.concatenate(coupled, 1)
    coupled = coupled + sum(swap(coupled, "row", rows, k) for k in range(1, rows))
    numbers = jnp.pad(
        update_map.astype(F32), ((0, nrhs - subs), (0, BLOCK - update_map.shape[1]))
    )
    coupled = jnp.concatenate([coupled, numbers], 1)
    near = jnp.stack(
        [coupled] + [swap(coupled, plane_axes, plane_size, CORES * m) for m in range(1, chips)]
    )
    far = swap(near, "col", cols, 1)

    shape = (leaves, rows, cols, lines)
    start = call(
        functools.partial(scatter_kernel, lines),
        jax.ShapeDtypeStruct((width // BLOCK, nrhs, BLOCK), F32),
        [WHOLE, WHOLE],
        4,
        (2 * nrhs * width, 12 * nrhs * width),
        (pltpu.SMEM((chips, subs, BLOCK), F32), pltpu.SemaphoreType.DMA((chips,))),
    )(near, sep_rhs)
    inside = sep_rows % BLOCK == 0
    own_width = rows * sep_rows
    length = subs * up + (own_width if inside else 0)
    piece = jax.ShapeDtypeStruct((chips, nrhs, length), F32)
    keep, send, *back = call(
        functools.partial(separator_kernel, shape, inside),
        (piece, piece) + (() if inside else (jax.ShapeDtypeStruct((nrhs, width), F32),)),
        [WHOLE] * 4,
        12,
        (4 * nrhs * sep_inverse.size, 4 * sep_inverse.size),
        (
            pltpu.VMEM((width // BLOCK, nrhs, BLOCK), F32),
            pltpu.VMEM(sep_inverse.shape, BF16),
            pltpu.VMEM(sep_inverse.shape, BF16),
            pltpu.SMEM((chips, subs, BLOCK), F32),
            pltpu.SMEM((chips, subs, BLOCK), F32),
            pltpu.SemaphoreType.DMA((chips,)),
            pltpu.SemaphoreType.DMA((chips,)),
        ),
    )(near, far, start, sep_inverse)
    if not inside:
        own = back[0].reshape(nrhs, leaves, rows, lines, CORES, sep_rows)
        own = own.transpose(4, 1, 3, 0, 2, 5).reshape(CORES, chips, nrhs, own_width)
        own = picked(picked(own, 0, core, CORES), 1, plane, chips)
        keep = jnp.concatenate([keep, own[0]], 2)
        send = jnp.concatenate([send, own[1]], 2)
    keep = keep + swap(send, "col", cols, 1)
    pulled = keep[0] + sum(swap(keep[m], plane_axes, plane_size, CORES * m) for m in range(1, chips))
    own = pulled[:, subs * up :]
    pulled = pulled[:, : subs * up]
    pulled = pulled + sum(swap(pulled, "row", rows, k) for k in range(1, rows))

    pull_other, pull_mine = (
        call(
            functools.partial(pull_kernel, first),
            vec,
            [WHOLE, WHOLE],
            12,
            (nrhs * update_rows.size, 2 * update_rows.size),
        )(pulled, update_rows)
        for first in (half, 0)
    )
    pull_mine = pull_mine + swap(pull_other, "col", cols, 1)
    pull_mine, pull_other = sum_over_lines(pull_mine, cols)
    share = leaf_cols // rows
    if inside and share % BLOCK == 0:
        near_part, far_parts = (
            call(
                functools.partial(solve_parts_kernel, rows, masks),
                (jax.ShapeDtypeStruct((nrhs, subs * share + sep_rows), F32),) * len(masks),
                [WHOLE] * 6,
                16,
                (leaf_flops * len(masks) // rows, 4 * leaf_inverse.size * len(masks) // rows),
            )(mine, other, pull_mine, pull_other, own, leaf_inverse)
            for masks in ((0,), tuple(range(1, rows)))
        )
        parts = [*near_part] + [swap(part, "row", rows, k) for k, part in enumerate(far_parts, 1)]
        return call(
            finish_kernel,
            (
                jax.ShapeDtypeStruct((subs, nrhs, share), F32),
                jax.ShapeDtypeStruct((nrhs, sep_rows), F32),
            ),
            [WHOLE] * rows,
            4,
            (parts[0].size * rows, 4 * parts[0].size * rows),
        )(*parts)
    terms = call(
        solve_kernel,
        jax.ShapeDtypeStruct((subs, nrhs, leaf_cols), F32),
        [WHOLE] * 5,
        16,
        (leaf_flops, 4 * leaf_inverse.size),
    )(mine, other, pull_mine, pull_other, leaf_inverse)

    def last(k):
        leaf_part = lax.dynamic_slice_in_dim(terms, (row ^ k) * share, share, 2)
        own_part = lax.dynamic_slice_in_dim(own, (row ^ k) * sep_rows, sep_rows, 1)
        return jnp.concatenate([*leaf_part, own_part], 1)

    parts = [last(0)] + [swap(last(k), "row", rows, k) for k in range(1, rows)]
    done = sum(parts[1:]) + parts[0]
    leaf_solution = jnp.stack([done[:, s * share : (s + 1) * share] for s in range(subs)])
    return (leaf_solution, done[:, subs * share :])


def solution(mesh):
    sizes = tuple(mesh.shape[a] for a in ("leaf", "row", "col"))
    in_specs = (
        P("leaf", None, "col"),
        P("leaf", "row", "col"),
        P("leaf", "col", "row"),
        P("leaf", None),
        P(),
        P(("leaf", "row", "col"), None),
    )
    out_specs = (P("leaf", None, ("col", "row")), P(None, ("leaf", "row", "col")))
    return jax.shard_map(
        functools.partial(body, sizes), mesh=mesh, in_specs=in_specs, out_specs=out_specs, check_vma=False
    )
```

```python
import functools

import jax
import jax.numpy as jnp
from jax import lax
from jax.experimental import pallas as pl
from jax.experimental.pallas import tpu as pltpu
from jax.sharding import PartitionSpec as P

BLOCK = 128
CORES = 2
MIB = 1 << 20

F32, BF16 = jnp.float32, jnp.bfloat16
HBM = pl.BlockSpec(memory_space=pltpu.HBM)
WHOLE = pl.BlockSpec(memory_space=pltpu.VMEM)


def in_hbm(value):
    return pltpu.with_memory_space_constraint(value, pltpu.HBM)


def in_vmem(value):
    return pltpu.with_memory_space_constraint(value, pltpu.VMEM)


def split(value):
    high = value.astype(BF16)
    return high, (value - high.astype(F32)).astype(BF16)


def dot3(value, halves, dims):
    rows = value.shape[0]
    high, low = halves
    parts = jnp.concatenate(split(value))
    main = lax.dot_general(parts, high, dims, preferred_element_type=F32)
    rest = lax.dot_general(parts[:rows], low, dims, preferred_element_type=F32)
    return main[:rows] + (main[rows:] + rest)


ROWS_OF = (((1,), (1,)), ((), ()))
COLUMNS_OF = (((1,), (0,)), ((), ()))


def role_of(col):
    for shift in (1, 2, 4, 8):
        col = col ^ (col >> shift)
    return col & 1


def sub_of(slot, half, role):
    return role * half + slot if slot < half else (1 - role) * half + (slot - half)


def chunk_of(rows):
    return min(rows, 512)


def leaf_kernel(rhs, inverse, mine, other, held, land, sems, rhs_sem):
    subs, rows, _ = inverse.shape
    half = subs // CORES
    role = role_of(lax.axis_index("col"))
    chunk = chunk_of(rows)
    steps = rows // chunk
    order = [*range(half, subs), *range(half)]

    def fetch(slot, step):
        part = pl.ds(step * chunk, chunk)
        return pltpu.make_async_copy(
            inverse.at[sub_of(slot, half, role), part], land.at[slot, part], sems.at[slot * steps + step]
        )

    first = pltpu.make_async_copy(rhs, held, rhs_sem)
    first.start()
    for slot in order:
        for step in range(steps):
            fetch(slot, step).start()
    first.wait()
    for slot in order:
        out, at = (mine, slot) if slot < half else (other, slot - half)
        value = held[sub_of(slot, half, role)]
        for step in range(steps):
            part = pl.ds(step * chunk, chunk)
            fetch(slot, step).wait()
            out[at, :, part] = dot3(value, split(land[slot, part]), ROWS_OF)


def couple_kernel(first, vectors, update, out):
    subs, up, _ = update.shape
    role = role_of(lax.axis_index("col"))
    for i in range(vectors.shape[0]):
        matrix = update[sub_of(first + i, subs // CORES, role)]
        out[:, i * up : (i + 1) * up] = dot3(vectors[i], split(matrix), ROWS_OF)


def load_kernel(value, out, sems):
    count = sems.shape[0]
    step = value.shape[0] // count
    copies = [
        pltpu.make_async_copy(
            value.at[pl.ds(i * step, step)], out.at[pl.ds(i * step, step)], sems.at[i]
        )
        for i in range(count)
    ]
    for copy in copies:
        copy.start()
    for copy in copies:
        copy.wait()


def numbers_of(pieces, numbers, sems):
    _, subs, _ = numbers.shape
    at = pieces.shape[2] - BLOCK
    return [
        pltpu.make_async_copy(
            pieces.at[chip, pl.ds(0, subs), pl.ds(at, BLOCK)], numbers.at[chip], sems.at[chip]
        )
        for chip in range(pieces.shape[0])
    ]


def core_of(col, side, chip):
    return (col + side + (chip > 0)) % CORES


def spots(lines, side, numbers, length):
    chips, subs, _ = numbers.shape
    here = length // (subs * BLOCK)
    me = lax.axis_index("col")
    for chip in range(chips):
        col = (me // CORES ^ (chip % lines)) * CORES + core_of(me, side, chip)
        role = role_of(col)
        for slot in range(subs):
            sub = sub_of(slot, subs // CORES, role)
            for k in range(here):
                at = (slot * here + k) * BLOCK
                block = numbers[chip, sub, col * here + k].astype(jnp.int32)
                yield chip, slice(at, at + BLOCK), block


def scatter_kernel(lines, near, rhs, out, numbers, sems):
    copies = numbers_of(near, numbers, sems)
    for copy in copies:
        copy.start()
    for b in range(out.shape[0]):
        out[b] = rhs[:, b * BLOCK : (b + 1) * BLOCK]
    for copy in copies:
        copy.wait()
    for chip, lanes, block in spots(lines, 0, numbers, near.shape[2] - BLOCK):
        out[block] -= near[chip, :, lanes]


def separator_kernel(sizes, inside, near, far, start, sep, keep, send, *rest):
    leaves, rows, cols, lines = sizes
    *back, held, high, low, ours, theirs, our_sems, their_sems = rest
    chips = far.shape[0]
    total = held.shape[0]
    length = far.shape[2] - BLOCK

    copies = numbers_of(far, theirs, their_sems) + numbers_of(near, ours, our_sems)
    for copy in copies:
        copy.start()
    held[...] = start[...]
    high[...], low[...] = split(sep[...])
    for copy in copies:
        copy.wait()
    for chip, lanes, block in spots(lines, 1, theirs, length):
        held[block] -= far[chip, :, lanes]
    updated = jnp.concatenate([held[b] for b in range(total)], 1)
    forward = dot3(updated, (high[...], low[...]), ROWS_OF)
    terms = dot3(forward, (high[...], low[...]), COLUMNS_OF)
    for b in range(total):
        held[b] = terms[:, b * BLOCK : (b + 1) * BLOCK]
    for side, numbers, out in ((1, theirs, send), (0, ours, keep)):
        for chip, lanes, block in spots(lines, side, numbers, length):
            out[chip, :, lanes] = held[block]
    if not inside:
        back[0][...] = terms
        return
    wide = sep.shape[0] // BLOCK
    me = lax.axis_index("col")
    plane = lax.axis_index("leaf") * lines + me // CORES
    for side, out in ((1, send), (0, keep)):
        for chip in range(chips):
            other = plane ^ chip
            col = (other % lines) * CORES + core_of(me, side, chip)
            for row in range(rows):
                for w in range(wide):
                    block = ((other // lines * rows + row) * cols + col) * wide + w
                    at = length + (row * wide + w) * BLOCK
                    out[chip, :, at : at + BLOCK] = held[block]


def pull_kernel(first, pulled, update, out):
    subs, up, _ = update.shape
    role = role_of(lax.axis_index("col"))
    for i in range(out.shape[0]):
        slot = first + i
        value = pulled[:, slot * up : (slot + 1) * up]
        matrix = update[sub_of(slot, subs // CORES, role)]
        out[i] = dot3(value, split(matrix), COLUMNS_OF)


def solve_kernel(mine, other, pull_mine, pull_other, inverse, out):
    half = mine.shape[0]
    role = role_of(lax.axis_index("col"))
    for slot in range(2 * half):
        if slot < half:
            value = mine[slot] - pull_mine[slot]
        else:
            value = other[slot - half] - pull_other[slot - half]
        sub = sub_of(slot, half, role)
        out[sub] = dot3(value, split(inverse[sub]), COLUMNS_OF)


def solve_parts_kernel(rows, masks, first, vectors, pull, own, inverse, *outs):
    half, width = vectors.shape[0], inverse.shape[2]
    share = width // rows
    sep_rows = own.shape[1] // rows
    row, role = lax.axis_index("row"), role_of(lax.axis_index("col"))
    for i in range(half):
        value = vectors[i] - pull[i]
        sub = sub_of(first + i, half, role)
        for mask, out in zip(masks, outs, strict=True):
            columns = pl.ds(pl.multiple_of((row ^ mask) * share, share), share)
            terms = dot3(value, split(inverse[sub, :, columns]), COLUMNS_OF)
            out[:, i * share : (i + 1) * share] = terms
    if first == 0:
        for mask, out in zip(masks, outs, strict=True):
            columns = pl.ds(pl.multiple_of((row ^ mask) * sep_rows, sep_rows), sep_rows)
            out[:, half * share :] = own[:, columns]


def finish_kernel(*refs):
    *parts, leaf_out, sep_out = refs
    subs, _, share = leaf_out.shape
    half, sep_rows = subs // CORES, sep_out.shape[1]
    role = role_of(lax.axis_index("col"))
    done = parts[0][...]
    for part in parts[1:]:
        done = done + part[...]
    for slot in range(subs):
        at = slot * share + (0 if slot < half else sep_rows)
        leaf_out[sub_of(slot, half, role)] = done[:, at : at + share]
    sep_out[...] = done[:, half * share : half * share + sep_rows]


def swap(value, axes, size, mask):
    return lax.ppermute(value, axes, [(i, i ^ mask) for i in range(size)])


def picked(value, dim, index, count):
    return jnp.stack(
        [lax.dynamic_index_in_dim(value, index ^ m, dim, keepdims=False) for m in range(count)], dim
    )


def beside(arrived, value):
    value = pl.pallas_call(
        load_kernel,
        out_shape=pltpu.VMEM(value.shape, value.dtype),
        in_specs=[HBM],
        out_specs=pl.BlockSpec(memory_space=pl.ANY),
        scratch_shapes=[pltpu.SemaphoreType.DMA((value.shape[0],))],
        compiler_params=pltpu.CompilerParams(vmem_limit_bytes=MIB),
        cost_estimate=pl.CostEstimate(flops=0, bytes_accessed=4 * value.size, transcendentals=0),
    )(in_hbm(value))
    return lax.optimization_barrier((arrived, value))


def sum_over_lines(mine, cols, arrived=None):
    step = CORES
    while step < cols:
        first = arrived is not None and step == CORES
        mine = mine + (arrived if first else swap(mine, "col", cols, step + 1))
        step *= 2
    return mine, swap(mine, "col", cols, 1)


def call(kernel, out_shape, in_specs, limit, cost, scratch=()):
    flops, nbytes = cost
    return pl.pallas_call(
        kernel,
        out_shape=out_shape,
        in_specs=in_specs,
        scratch_shapes=scratch,
        compiler_params=pltpu.CompilerParams(vmem_limit_bytes=limit * MIB),
        cost_estimate=pl.CostEstimate(flops=flops, bytes_accessed=nbytes, transcendentals=0),
    )


def body(sizes, leaf_rhs, leaf_inverse, update_rows, update_map, sep_rhs, sep_inverse):
    leaves, rows, cols = sizes
    lines = cols // CORES
    chips = leaves * lines
    subs, nrhs, _ = leaf_rhs.shape
    half = subs // CORES
    width = sep_rhs.shape[1]
    sep_rows = sep_inverse.shape[0]
    _, leaf_rows, leaf_cols = leaf_inverse.shape
    up = update_rows.shape[1]
    leaf, row, col = (lax.axis_index(a) for a in ("leaf", "row", "col"))
    core, line = col % CORES, col // CORES
    plane = leaf * lines + line
    plane_axes, plane_size = ("leaf", "col"), leaves * cols

    vec = jax.ShapeDtypeStruct((half, nrhs, leaf_rows), F32)
    leaf_flops = 2 * nrhs * leaf_inverse.size
    mine, other = call(
        leaf_kernel,
        (pltpu.VMEM(vec.shape, F32), pltpu.VMEM(vec.shape, F32)),
        [HBM, HBM],
        61,
        (leaf_flops, 4 * leaf_inverse.size),
        (
            pltpu.VMEM(leaf_rhs.shape, F32),
            pltpu.VMEM(leaf_inverse.shape, F32),
            pltpu.SemaphoreType.DMA((subs * (leaf_rows // chunk_of(leaf_rows)),)),
            pltpu.SemaphoreType.DMA,
        ),
    )(in_hbm(leaf_rhs), in_hbm(leaf_inverse))

    mine = mine + swap(other, "col", cols, 1)
    arrived, update = beside(swap(mine, "col", cols, CORES + 1), update_rows)
    mine, other = sum_over_lines(mine, cols, arrived)
    coupled = [
        call(
            functools.partial(couple_kernel, first),
            jax.ShapeDtypeStruct((nrhs, half * up), F32),
            [WHOLE, WHOLE],
            12,
            (nrhs * update_rows.size, 2 * update_rows.size),
        )(vectors, in_vmem(update))
        for first, vectors in ((0, mine), (half, other))
    ]
    coupled = jnp.concatenate(coupled, 1)
    coupled = coupled + sum(swap(coupled, "row", rows, k) for k in range(1, rows))
    numbers = jnp.pad(
        update_map.astype(F32), ((0, nrhs - subs), (0, BLOCK - update_map.shape[1]))
    )
    coupled = jnp.concatenate([coupled, numbers], 1)
    near = jnp.stack(
        [coupled] + [swap(coupled, plane_axes, plane_size, CORES * m + 1) for m in range(1, chips)]
    )
    far = swap(near, "col", cols, 1)

    shape = (leaves, rows, cols, lines)
    start = call(
        functools.partial(scatter_kernel, lines),
        jax.ShapeDtypeStruct((width // BLOCK, nrhs, BLOCK), F32),
        [WHOLE, WHOLE],
        4,
        (2 * nrhs * width, 12 * nrhs * width),
        (pltpu.SMEM((chips, subs, BLOCK), F32), pltpu.SemaphoreType.DMA((chips,))),
    )(near, sep_rhs)
    inside = sep_rows % BLOCK == 0
    own_width = rows * sep_rows
    length = subs * up + (own_width if inside else 0)
    piece = jax.ShapeDtypeStruct((chips, nrhs, length), F32)
    keep, send, *back = call(
        functools.partial(separator_kernel, shape, inside),
        (piece, piece) + (() if inside else (jax.ShapeDtypeStruct((nrhs, width), F32),)),
        [WHOLE] * 4,
        12,
        (4 * nrhs * sep_inverse.size, 4 * sep_inverse.size),
        (
            pltpu.VMEM((width // BLOCK, nrhs, BLOCK), F32),
            pltpu.VMEM(sep_inverse.shape, BF16),
            pltpu.VMEM(sep_inverse.shape, BF16),
            pltpu.SMEM((chips, subs, BLOCK), F32),
            pltpu.SMEM((chips, subs, BLOCK), F32),
            pltpu.SemaphoreType.DMA((chips,)),
            pltpu.SemaphoreType.DMA((chips,)),
        ),
    )(near, far, start, sep_inverse)
    if not inside:
        own = back[0].reshape(nrhs, leaves, rows, lines, CORES, sep_rows)
        own = own.transpose(4, 1, 3, 0, 2, 5).reshape(CORES, chips, nrhs, own_width)
        own = picked(picked(own, 0, core, CORES), 1, plane, chips)
        own = [jnp.concatenate([own[i][:1], own[1 - i][1:]]) for i in range(CORES)]
        keep = jnp.concatenate([keep, own[0]], 2)
        send = jnp.concatenate([send, own[1]], 2)
    keep = keep + swap(send, "col", cols, 1)
    pulled = keep[0] + sum(swap(keep[m], plane_axes, plane_size, CORES * m + 1) for m in range(1, chips))
    own = pulled[:, subs * up :]
    pulled = pulled[:, : subs * up]
    pulled = pulled + sum(swap(pulled, "row", rows, k) for k in range(1, rows))

    pull_other, pull_mine = (
        call(
            functools.partial(pull_kernel, first),
            vec,
            [WHOLE, WHOLE],
            12,
            (nrhs * update_rows.size, 2 * update_rows.size),
        )(pulled, update_rows)
        for first in (half, 0)
    )
    pull_mine = pull_mine + swap(pull_other, "col", cols, 1)
    pull_mine, pull_other = sum_over_lines(pull_mine, cols)
    share = leaf_cols // rows
    if inside and share % BLOCK == 0:
        def parts_of(masks):
            halves = [
                call(
                    functools.partial(solve_parts_kernel, rows, masks, first),
                    (jax.ShapeDtypeStruct((nrhs, half * share + (0 if first else sep_rows)), F32),)
                    * len(masks),
                    [WHOLE] * 4,
                    16,
                    (leaf_flops * len(masks) // (2 * rows), 2 * leaf_inverse.size * len(masks) // rows),
                )(vectors, pull, own, leaf_inverse)
                for first, vectors, pull in ((0, mine, pull_mine), (half, other, pull_other))
            ]
            return [jnp.concatenate(pair, 1) for pair in zip(*halves, strict=True)]

        far_parts = [swap(part, "row", rows, k) for k, part in enumerate(parts_of(tuple(range(1, rows))), 1)]
        parts = parts_of((0,)) + far_parts
        return call(
            finish_kernel,
            (
                jax.ShapeDtypeStruct((subs, nrhs, share), F32),
                jax.ShapeDtypeStruct((nrhs, sep_rows), F32),
            ),
            [WHOLE] * rows,
            4,
            (parts[0].size * rows, 4 * parts[0].size * rows),
        )(*parts)
    terms = call(
        solve_kernel,
        jax.ShapeDtypeStruct((subs, nrhs, leaf_cols), F32),
        [WHOLE] * 5,
        16,
        (leaf_flops, 4 * leaf_inverse.size),
    )(mine, other, pull_mine, pull_other, leaf_inverse)

    def last(k):
        leaf_part = lax.dynamic_slice_in_dim(terms, (row ^ k) * share, share, 2)
        own_part = lax.dynamic_slice_in_dim(own, (row ^ k) * sep_rows, sep_rows, 1)
        return jnp.concatenate([*leaf_part, own_part], 1)

    parts = [last(0)] + [swap(last(k), "row", rows, k) for k in range(1, rows)]
    done = sum(parts[1:]) + parts[0]
    leaf_solution = jnp.stack([done[:, s * share : (s + 1) * share] for s in range(subs)])
    return (leaf_solution, done[:, subs * share :])


def solution(mesh):
    sizes = tuple(mesh.shape[a] for a in ("leaf", "row", "col"))
    in_specs = (
        P("leaf", None, "col"),
        P("leaf", "row", "col"),
        P("leaf", "col", "row"),
        P("leaf", None),
        P(),
        P(("leaf", "row", "col"), None),
    )
    out_specs = (P("leaf", None, ("col", "row")), P(None, ("leaf", "row", "col")))
    return jax.shard_map(
        functools.partial(body, sizes), mesh=mesh, in_specs=in_specs, out_specs=out_specs, check_vma=False
    )
```

```python
import functools

import jax
import jax.numpy as jnp
from jax import lax
from jax.experimental import pallas as pl
from jax.experimental.pallas import tpu as pltpu
from jax.sharding import PartitionSpec as P

BLOCK = 128
CORES = 2
MIB = 1 << 20

F32, BF16 = jnp.float32, jnp.bfloat16
HBM = pl.BlockSpec(memory_space=pltpu.HBM)
SCALARS = pl.BlockSpec(memory_space=pltpu.SMEM)
WHOLE = pl.BlockSpec(memory_space=pltpu.VMEM)


def in_hbm(value):
    return pltpu.with_memory_space_constraint(value, pltpu.HBM)


def in_vmem(value):
    return pltpu.with_memory_space_constraint(value, pltpu.VMEM)


def split(value):
    high = value.astype(BF16)
    return high, (value - high.astype(F32)).astype(BF16)


def dot3(value, halves, dims):
    rows = value.shape[0]
    high, low = halves
    parts = jnp.concatenate(split(value))
    main = lax.dot_general(parts, high, dims, preferred_element_type=F32)
    rest = lax.dot_general(parts[:rows], low, dims, preferred_element_type=F32)
    return main[:rows] + (main[rows:] + rest)


ROWS_OF = (((1,), (1,)), ((), ()))
COLUMNS_OF = (((1,), (0,)), ((), ()))


def role_of(col):
    for shift in (1, 2, 4, 8):
        col = col ^ (col >> shift)
    return col & 1


def sub_of(slot, half, role):
    return role * half + slot if slot < half else (1 - role) * half + (slot - half)


def chunk_of(rows):
    return min(rows, 512)


def leaf_kernel(rhs, inverse, mine, other, held, land, sems, rhs_sem):
    subs, rows, _ = inverse.shape
    half = subs // CORES
    role = role_of(lax.axis_index("col"))
    chunk = chunk_of(rows)
    steps = rows // chunk
    order = [*range(half, subs), *range(half)]

    def fetch(slot, step):
        part = pl.ds(step * chunk, chunk)
        return pltpu.make_async_copy(
            inverse.at[sub_of(slot, half, role), part], land.at[slot, part], sems.at[slot * steps + step]
        )

    first = pltpu.make_async_copy(rhs, held, rhs_sem)
    first.start()
    for slot in order:
        for step in range(steps):
            fetch(slot, step).start()
    first.wait()
    for slot in order:
        out, at = (mine, slot) if slot < half else (other, slot - half)
        value = held[sub_of(slot, half, role)]
        for step in range(steps):
            part = pl.ds(step * chunk, chunk)
            fetch(slot, step).wait()
            out[at, :, part] = dot3(value, split(land[slot, part]), ROWS_OF)


def couple_kernel(first, vectors, update, out):
    subs, up, _ = update.shape
    role = role_of(lax.axis_index("col"))
    for i in range(vectors.shape[0]):
        matrix = update[sub_of(first + i, subs // CORES, role)]
        out[:, i * up : (i + 1) * up] = dot3(vectors[i], split(matrix), ROWS_OF)


def load_kernel(value, out, sems):
    count = sems.shape[0]
    step = value.shape[0] // count
    copies = [
        pltpu.make_async_copy(
            value.at[pl.ds(i * step, step)], out.at[pl.ds(i * step, step)], sems.at[i]
        )
        for i in range(count)
    ]
    for copy in copies:
        copy.start()
    for copy in copies:
        copy.wait()


def numbers_of(pieces, numbers, sems):
    _, subs, _ = numbers.shape
    at = pieces.shape[2] - BLOCK
    return [
        pltpu.make_async_copy(
            pieces.at[chip, pl.ds(0, subs), pl.ds(at, BLOCK)], numbers.at[chip], sems.at[chip]
        )
        for chip in range(pieces.shape[0])
    ]


def core_of(col, side, chip):
    return (col + side + (chip > 0)) % CORES


def spots(table, side, chips, length):
    count = length // BLOCK
    for chip in range(chips):
        for k in range(count):
            yield chip, slice(k * BLOCK, (k + 1) * BLOCK), table[side, chip * count + k]


def scatter_kernel(lines, near, rhs, out, table, numbers, sems):
    chips, _, length = near.shape
    length -= BLOCK
    subs = numbers.shape[1]
    here = length // (subs * BLOCK)
    me = lax.axis_index("col")
    copies = numbers_of(near, numbers, sems)
    for copy in copies:
        copy.start()
    for b in range(out.shape[0]):
        out[b] = rhs[:, b * BLOCK : (b + 1) * BLOCK]
    for copy in copies:
        copy.wait()
    for side in range(CORES):
        for chip in range(chips):
            col = (me // CORES ^ (chip % lines)) * CORES + core_of(me, side, chip)
            role = role_of(col)
            for slot in range(subs):
                sub = sub_of(slot, subs // CORES, role)
                for k in range(here):
                    block = numbers[chip, sub, col * here + k].astype(jnp.int32)
                    table[side, (chip * subs + slot) * here + k] = block
    for chip, lanes, block in spots(table, 0, chips, length):
        out[block] -= near[chip, :, lanes]


def prepare_kernel(inside, sep, both, *rest):
    *tall, land, sem = rest
    rows = sep.shape[0]
    copy = pltpu.make_async_copy(sep, land, sem)
    copy.start()
    copy.wait()
    both[:rows], both[rows:] = split(land[...])
    if inside:
        tall[0][:, :rows], tall[0][:, rows:] = split(land[...].T)


def separator_kernel(sizes, inside, table, far, start, both, *rest):
    *tall, send, held = rest
    chips, nrhs, length = far.shape
    length -= BLOCK
    total = held.shape[0]
    sep_rows = both.shape[0] // 2

    held[...] = start[...]
    for chip, lanes, block in spots(table, 1, chips, length):
        held[block] -= far[chip, :, lanes]
    updated = jnp.concatenate(split(jnp.concatenate([held[b] for b in range(total)], 1)))
    matrix, dims = (tall[0], COLUMNS_OF) if inside else (both, ROWS_OF)
    forward = lax.dot_general(updated, matrix[...], dims, preferred_element_type=F32)
    forward = forward[:nrhs, :sep_rows] + (forward[nrhs:, :sep_rows] + forward[:nrhs, sep_rows:])
    high, low = split(forward)
    parts = jnp.concatenate(
        [jnp.concatenate([high, high], 1), jnp.concatenate([low, jnp.zeros_like(low)], 1)]
    )
    terms = lax.dot_general(parts, both[...], COLUMNS_OF, preferred_element_type=F32)
    terms = terms[:nrhs] + terms[nrhs:]
    for b in range(total):
        held[b] = terms[:, b * BLOCK : (b + 1) * BLOCK]
    pick(sizes, 1, inside, sep_rows, table, held, length, send)


def keep_kernel(sizes, inside, sep_rows, length, table, held, keep):
    pick(sizes, 0, inside, sep_rows, table, held, length, keep)


def pick(sizes, side, inside, sep_rows, table, held, length, out):
    _, rows, cols, lines = sizes
    for chip, lanes, block in spots(table, side, out.shape[0], length):
        out[chip, :, lanes] = held[block]
    if not inside:
        return
    wide = sep_rows // BLOCK
    me = lax.axis_index("col")
    plane = lax.axis_index("leaf") * lines + me // CORES
    for chip in range(out.shape[0]):
        other = plane ^ chip
        col = (other % lines) * CORES + core_of(me, side, chip)
        for row in range(rows):
            for w in range(wide):
                block = ((other // lines * rows + row) * cols + col) * wide + w
                at = length + (row * wide + w) * BLOCK
                out[chip, :, at : at + BLOCK] = held[block]


def pull_kernel(first, pulled, update, out):
    subs, up, _ = update.shape
    role = role_of(lax.axis_index("col"))
    for i in range(out.shape[0]):
        slot = first + i
        value = pulled[:, slot * up : (slot + 1) * up]
        matrix = update[sub_of(slot, subs // CORES, role)]
        out[i] = dot3(value, split(matrix), COLUMNS_OF)


def solve_kernel(mine, other, pull_mine, pull_other, inverse, out):
    half = mine.shape[0]
    role = role_of(lax.axis_index("col"))
    for slot in range(2 * half):
        if slot < half:
            value = mine[slot] - pull_mine[slot]
        else:
            value = other[slot - half] - pull_other[slot - half]
        sub = sub_of(slot, half, role)
        out[sub] = dot3(value, split(inverse[sub]), COLUMNS_OF)


def solve_parts_kernel(rows, masks, first, vectors, pull, own, inverse, *outs):
    half, width = vectors.shape[0], inverse.shape[2]
    share = width // rows
    sep_rows = own.shape[1] // rows
    row, role = lax.axis_index("row"), role_of(lax.axis_index("col"))
    for i in range(half):
        value = vectors[i] - pull[i]
        sub = sub_of(first + i, half, role)
        for mask, out in zip(masks, outs, strict=True):
            columns = pl.ds(pl.multiple_of((row ^ mask) * share, share), share)
            terms = dot3(value, split(inverse[sub, :, columns]), COLUMNS_OF)
            out[:, i * share : (i + 1) * share] = terms
    if first == 0:
        for mask, out in zip(masks, outs, strict=True):
            columns = pl.ds(pl.multiple_of((row ^ mask) * sep_rows, sep_rows), sep_rows)
            out[:, half * share :] = own[:, columns]


def finish_kernel(*refs):
    *parts, leaf_out, sep_out = refs
    subs, _, share = leaf_out.shape
    half, sep_rows = subs // CORES, sep_out.shape[1]
    role = role_of(lax.axis_index("col"))
    done = parts[0][...]
    for part in parts[1:]:
        done = done + part[...]
    for slot in range(subs):
        at = slot * share + (0 if slot < half else sep_rows)
        leaf_out[sub_of(slot, half, role)] = done[:, at : at + share]
    sep_out[...] = done[:, half * share : half * share + sep_rows]


def swap(value, axes, size, mask):
    return lax.ppermute(value, axes, [(i, i ^ mask) for i in range(size)])


def picked(value, dim, index, count):
    return jnp.stack(
        [lax.dynamic_index_in_dim(value, index ^ m, dim, keepdims=False) for m in range(count)], dim
    )


def beside(arrived, value):
    value = pl.pallas_call(
        load_kernel,
        out_shape=pltpu.VMEM(value.shape, value.dtype),
        in_specs=[HBM],
        out_specs=pl.BlockSpec(memory_space=pl.ANY),
        scratch_shapes=[pltpu.SemaphoreType.DMA((value.shape[0],))],
        compiler_params=pltpu.CompilerParams(vmem_limit_bytes=MIB),
        cost_estimate=pl.CostEstimate(flops=0, bytes_accessed=4 * value.size, transcendentals=0),
    )(in_hbm(value))
    return lax.optimization_barrier((arrived, value))


def sum_over_lines(mine, cols, arrived=None):
    step = CORES
    while step < cols:
        first = arrived is not None and step == CORES
        mine = mine + (arrived if first else swap(mine, "col", cols, step + 1))
        step *= 2
    return mine, swap(mine, "col", cols, 1)


def call(kernel, out_shape, in_specs, limit, cost, scratch=()):
    flops, nbytes = cost
    return pl.pallas_call(
        kernel,
        out_shape=out_shape,
        in_specs=in_specs,
        scratch_shapes=scratch,
        compiler_params=pltpu.CompilerParams(vmem_limit_bytes=limit * MIB),
        cost_estimate=pl.CostEstimate(flops=flops, bytes_accessed=nbytes, transcendentals=0),
    )


def body(sizes, leaf_rhs, leaf_inverse, update_rows, update_map, sep_rhs, sep_inverse):
    leaves, rows, cols = sizes
    lines = cols // CORES
    chips = leaves * lines
    subs, nrhs, _ = leaf_rhs.shape
    half = subs // CORES
    width = sep_rhs.shape[1]
    sep_rows = sep_inverse.shape[0]
    _, leaf_rows, leaf_cols = leaf_inverse.shape
    up = update_rows.shape[1]
    leaf, row, col = (lax.axis_index(a) for a in ("leaf", "row", "col"))
    core, line = col % CORES, col // CORES
    plane = leaf * lines + line
    plane_axes, plane_size = ("leaf", "col"), leaves * cols

    vec = jax.ShapeDtypeStruct((half, nrhs, leaf_rows), F32)
    leaf_flops = 2 * nrhs * leaf_inverse.size
    mine, other = call(
        leaf_kernel,
        (pltpu.VMEM(vec.shape, F32), pltpu.VMEM(vec.shape, F32)),
        [HBM, HBM],
        61,
        (leaf_flops, 4 * leaf_inverse.size),
        (
            pltpu.VMEM(leaf_rhs.shape, F32),
            pltpu.VMEM(leaf_inverse.shape, F32),
            pltpu.SemaphoreType.DMA((subs * (leaf_rows // chunk_of(leaf_rows)),)),
            pltpu.SemaphoreType.DMA,
        ),
    )(in_hbm(leaf_rhs), in_hbm(leaf_inverse))

    mine = mine + swap(other, "col", cols, 1)
    arrived, update = beside(swap(mine, "col", cols, CORES + 1), update_rows)
    mine, other = sum_over_lines(mine, cols, arrived)
    coupled = [
        call(
            functools.partial(couple_kernel, first),
            jax.ShapeDtypeStruct((nrhs, half * up), F32),
            [WHOLE, WHOLE],
            12,
            (nrhs * update_rows.size, 2 * update_rows.size),
        )(vectors, in_vmem(update))
        for first, vectors in ((0, mine), (half, other))
    ]
    coupled = jnp.concatenate(coupled, 1)
    arrived = [swap(coupled, "row", rows, k) for k in range(1, rows)]
    inside = sep_rows % BLOCK == 0
    prepared = pl.pallas_call(
        functools.partial(prepare_kernel, inside),
        out_shape=[pltpu.VMEM((2 * sep_rows, width), BF16)]
        + ([pltpu.VMEM((width, 2 * sep_rows), BF16)] if inside else []),
        in_specs=[HBM],
        scratch_shapes=[pltpu.VMEM(sep_inverse.shape, F32), pltpu.SemaphoreType.DMA],
        compiler_params=pltpu.CompilerParams(vmem_limit_bytes=12 * MIB),
        cost_estimate=pl.CostEstimate(
            flops=0, bytes_accessed=8 * sep_inverse.size, transcendentals=0
        ),
    )(in_hbm(sep_inverse))
    arrived, prepared = lax.optimization_barrier((arrived, prepared))
    coupled = coupled + sum(arrived)
    numbers = jnp.pad(
        update_map.astype(F32), ((0, nrhs - subs), (0, BLOCK - update_map.shape[1]))
    )
    coupled = jnp.concatenate([coupled, numbers], 1)
    near = jnp.stack(
        [coupled] + [swap(coupled, plane_axes, plane_size, CORES * m + 1) for m in range(1, chips)]
    )
    far = swap(near, "col", cols, 1)

    shape = (leaves, rows, cols, lines)
    size = subs * up
    start, table = pl.pallas_call(
        functools.partial(scatter_kernel, lines),
        out_shape=[
            jax.ShapeDtypeStruct((width // BLOCK, nrhs, BLOCK), F32),
            pltpu.SMEM((CORES, chips * size // BLOCK), jnp.int32),
        ],
        in_specs=[WHOLE, WHOLE],
        out_specs=[WHOLE, SCALARS],
        scratch_shapes=[pltpu.SMEM((chips, subs, BLOCK), F32), pltpu.SemaphoreType.DMA((chips,))],
        compiler_params=pltpu.CompilerParams(vmem_limit_bytes=4 * MIB),
        cost_estimate=pl.CostEstimate(
            flops=2 * nrhs * width, bytes_accessed=12 * nrhs * width, transcendentals=0
        ),
    )(near, sep_rhs)
    table = pltpu.with_memory_space_constraint(table, pltpu.SMEM)
    own_width = rows * sep_rows
    length = size + (own_width if inside else 0)
    piece = jax.ShapeDtypeStruct((chips, nrhs, length), F32)
    send, held = call(
        functools.partial(separator_kernel, shape, inside),
        (piece, jax.ShapeDtypeStruct((width // BLOCK, nrhs, BLOCK), F32)),
        [SCALARS] + [WHOLE] * (2 + len(prepared)),
        12,
        (4 * nrhs * sep_inverse.size, 4 * sep_inverse.size),
    )(table, far, start, *map(in_vmem, prepared))
    keep = call(
        functools.partial(keep_kernel, shape, inside, sep_rows, size),
        piece,
        [SCALARS, WHOLE],
        4,
        (0, 8 * piece.size),
    )(table, held)
    if not inside:
        own = held.transpose(1, 0, 2).reshape(nrhs, leaves, rows, lines, CORES, sep_rows)
        own = own.transpose(4, 1, 3, 0, 2, 5).reshape(CORES, chips, nrhs, own_width)
        own = picked(picked(own, 0, core, CORES), 1, plane, chips)
        own = [jnp.concatenate([own[i][:1], own[1 - i][1:]]) for i in range(CORES)]
        keep = jnp.concatenate([keep, own[0]], 2)
        send = jnp.concatenate([send, own[1]], 2)
    keep = keep + swap(send, "col", cols, 1)
    pulled = keep[0] + sum(swap(keep[m], plane_axes, plane_size, CORES * m + 1) for m in range(1, chips))
    own = pulled[:, subs * up :]
    pulled = pulled[:, : subs * up]
    pulled = pulled + sum(swap(pulled, "row", rows, k) for k in range(1, rows))

    pull_other, pull_mine = (
        call(
            functools.partial(pull_kernel, first),
            vec,
            [WHOLE, WHOLE],
            12,
            (nrhs * update_rows.size, 2 * update_rows.size),
        )(pulled, update_rows)
        for first in (half, 0)
    )
    pull_mine = pull_mine + swap(pull_other, "col", cols, 1)
    pull_mine, pull_other = sum_over_lines(pull_mine, cols)
    share = leaf_cols // rows
    if inside and share % BLOCK == 0:
        def parts_of(masks):
            halves = [
                call(
                    functools.partial(solve_parts_kernel, rows, masks, first),
                    (jax.ShapeDtypeStruct((nrhs, half * share + (0 if first else sep_rows)), F32),)
                    * len(masks),
                    [WHOLE] * 4,
                    16,
                    (leaf_flops * len(masks) // (2 * rows), 2 * leaf_inverse.size * len(masks) // rows),
                )(vectors, pull, own, leaf_inverse)
                for first, vectors, pull in ((0, mine, pull_mine), (half, other, pull_other))
            ]
            return [jnp.concatenate(pair, 1) for pair in zip(*halves, strict=True)]

        far_parts = [swap(part, "row", rows, k) for k, part in enumerate(parts_of(tuple(range(1, rows))), 1)]
        parts = parts_of((0,)) + far_parts
        return call(
            finish_kernel,
            (
                jax.ShapeDtypeStruct((subs, nrhs, share), F32),
                jax.ShapeDtypeStruct((nrhs, sep_rows), F32),
            ),
            [WHOLE] * rows,
            4,
            (parts[0].size * rows, 4 * parts[0].size * rows),
        )(*parts)
    terms = call(
        solve_kernel,
        jax.ShapeDtypeStruct((subs, nrhs, leaf_cols), F32),
        [WHOLE] * 5,
        16,
        (leaf_flops, 4 * leaf_inverse.size),
    )(mine, other, pull_mine, pull_other, leaf_inverse)

    def last(k):
        leaf_part = lax.dynamic_slice_in_dim(terms, (row ^ k) * share, share, 2)
        own_part = lax.dynamic_slice_in_dim(own, (row ^ k) * sep_rows, sep_rows, 1)
        return jnp.concatenate([*leaf_part, own_part], 1)

    parts = [last(0)] + [swap(last(k), "row", rows, k) for k in range(1, rows)]
    done = sum(parts[1:]) + parts[0]
    leaf_solution = jnp.stack([done[:, s * share : (s + 1) * share] for s in range(subs)])
    return (leaf_solution, done[:, subs * share :])


def solution(mesh):
    sizes = tuple(mesh.shape[a] for a in ("leaf", "row", "col"))
    in_specs = (
        P("leaf", None, "col"),
        P("leaf", "row", "col"),
        P("leaf", "col", "row"),
        P("leaf", None),
        P(),
        P(("leaf", "row", "col"), None),
    )
    out_specs = (P("leaf", None, ("col", "row")), P(None, ("leaf", "row", "col")))
    return jax.shard_map(
        functools.partial(body, sizes), mesh=mesh, in_specs=in_specs, out_specs=out_specs, check_vma=False
    )
```

```python
import functools

import jax
import jax.numpy as jnp
from jax import lax
from jax.experimental import pallas as pl
from jax.experimental.pallas import tpu as pltpu
from jax.sharding import PartitionSpec as P

BLOCK = 128
CORES = 2
MIB = 1 << 20
LIMIT = 56

F32, BF16 = jnp.float32, jnp.bfloat16
HBM = pl.BlockSpec(memory_space=pltpu.HBM)
SCALARS = pl.BlockSpec(memory_space=pltpu.SMEM)
WHOLE = pl.BlockSpec(memory_space=pltpu.VMEM)


def in_hbm(value):
    return pltpu.with_memory_space_constraint(value, pltpu.HBM)


def in_vmem(value):
    return pltpu.with_memory_space_constraint(value, pltpu.VMEM)


def split(value):
    high = value.astype(BF16)
    return high, (value - high.astype(F32)).astype(BF16)


def dot3(value, halves, dims):
    rows = value.shape[0]
    high, low = halves
    parts = jnp.concatenate(split(value))
    main = lax.dot_general(parts, high, dims, preferred_element_type=F32)
    rest = lax.dot_general(parts[:rows], low, dims, preferred_element_type=F32)
    return main[:rows] + (main[rows:] + rest)


ROWS_OF = (((1,), (1,)), ((), ()))
COLUMNS_OF = (((1,), (0,)), ((), ()))


def role_of(col):
    for shift in (1, 2, 4, 8):
        col = col ^ (col >> shift)
    return col & 1


def sub_of(slot, half, role):
    return role * half + slot if slot < half else (1 - role) * half + (slot - half)


def chunk_of(rows):
    return min(rows, 512)


def leaf_kernel(rhs, inverse, other, kept, held, land, sems, rhs_sem):
    half, rows, _ = land.shape
    role = role_of(lax.axis_index("col"))
    chunk = chunk_of(rows)
    steps = rows // chunk

    def fetch(slot, step):
        part = pl.ds(step * chunk, chunk)
        into = kept.at[slot] if slot < half else land.at[slot - half]
        return pltpu.make_async_copy(
            inverse.at[sub_of(slot, half, role), part], into.at[part], sems.at[slot * steps + step]
        )

    first = pltpu.make_async_copy(rhs, held, rhs_sem)
    first.start()
    for slot in [*range(half, 2 * half), *range(half)]:
        for step in range(steps):
            fetch(slot, step).start()
    first.wait()
    for slot in range(half, 2 * half):
        value = held[sub_of(slot, half, role)]
        for step in range(steps):
            part = pl.ds(step * chunk, chunk)
            fetch(slot, step).wait()
            other[slot - half, :, part] = dot3(value, split(land[slot - half, part]), ROWS_OF)
    for slot in range(half):
        for step in range(steps):
            fetch(slot, step).wait()


def rest_kernel(rhs, kept, mine):
    half = kept.shape[0]
    role = role_of(lax.axis_index("col"))
    for slot in range(half):
        mine[slot] = dot3(rhs[sub_of(slot, half, role)], split(kept[slot]), ROWS_OF)


def couple_kernel(first, vectors, update, out):
    subs, up, _ = update.shape
    role = role_of(lax.axis_index("col"))
    for i in range(vectors.shape[0]):
        matrix = update[sub_of(first + i, subs // CORES, role)]
        out[:, i * up : (i + 1) * up] = dot3(vectors[i], split(matrix), ROWS_OF)


def load_kernel(value, out, sems):
    count = sems.shape[0]
    step = value.shape[0] // count
    copies = [
        pltpu.make_async_copy(
            value.at[pl.ds(i * step, step)], out.at[pl.ds(i * step, step)], sems.at[i]
        )
        for i in range(count)
    ]
    for copy in copies:
        copy.start()
    for copy in copies:
        copy.wait()


def numbers_of(pieces, numbers, sems):
    _, subs, _ = numbers.shape
    at = pieces.shape[2] - BLOCK
    return [
        pltpu.make_async_copy(
            pieces.at[chip, pl.ds(0, subs), pl.ds(at, BLOCK)], numbers.at[chip], sems.at[chip]
        )
        for chip in range(pieces.shape[0])
    ]


def core_of(col, side, chip):
    return (col + side + (chip > 0)) % CORES


def spots(table, side, chips, length):
    count = length // BLOCK
    for chip in range(chips):
        for k in range(count):
            yield chip, slice(k * BLOCK, (k + 1) * BLOCK), table[side, chip * count + k]


def scatter_kernel(lines, near, rhs, out, table, numbers, sems):
    chips, _, length = near.shape
    length -= BLOCK
    subs = numbers.shape[1]
    here = length // (subs * BLOCK)
    me = lax.axis_index("col")
    copies = numbers_of(near, numbers, sems)
    for copy in copies:
        copy.start()
    for b in range(out.shape[0]):
        out[b] = rhs[:, b * BLOCK : (b + 1) * BLOCK]
    for copy in copies:
        copy.wait()
    for side in range(CORES):
        for chip in range(chips):
            col = (me // CORES ^ (chip % lines)) * CORES + core_of(me, side, chip)
            role = role_of(col)
            for slot in range(subs):
                sub = sub_of(slot, subs // CORES, role)
                for k in range(here):
                    block = numbers[chip, sub, col * here + k].astype(jnp.int32)
                    table[side, (chip * subs + slot) * here + k] = block
    for chip, lanes, block in spots(table, 0, chips, length):
        out[block] -= near[chip, :, lanes]


def prepare_kernel(inside, sep, both, *rest):
    *tall, land, sem = rest
    rows = sep.shape[0]
    copy = pltpu.make_async_copy(sep, land, sem)
    copy.start()
    copy.wait()
    both[:rows], both[rows:] = split(land[...])
    if inside:
        tall[0][:, :rows], tall[0][:, rows:] = split(land[...].T)


def separator_kernel(sizes, inside, table, far, start, both, *rest):
    *tall, send, held = rest
    chips, nrhs, length = far.shape
    length -= BLOCK
    total = held.shape[0]
    sep_rows = both.shape[0] // 2

    held[...] = start[...]
    for chip, lanes, block in spots(table, 1, chips, length):
        held[block] -= far[chip, :, lanes]
    updated = jnp.concatenate(split(jnp.concatenate([held[b] for b in range(total)], 1)))
    matrix, dims = (tall[0], COLUMNS_OF) if inside else (both, ROWS_OF)
    forward = lax.dot_general(updated, matrix[...], dims, preferred_element_type=F32)
    forward = forward[:nrhs, :sep_rows] + (forward[nrhs:, :sep_rows] + forward[:nrhs, sep_rows:])
    high, low = split(forward)
    parts = jnp.concatenate(
        [jnp.concatenate([high, high], 1), jnp.concatenate([low, jnp.zeros_like(low)], 1)]
    )
    terms = lax.dot_general(parts, both[...], COLUMNS_OF, preferred_element_type=F32)
    terms = terms[:nrhs] + terms[nrhs:]
    for b in range(total):
        held[b] = terms[:, b * BLOCK : (b + 1) * BLOCK]
    pick(sizes, 1, inside, sep_rows, table, held, length, send)


def keep_kernel(sizes, inside, sep_rows, length, table, held, keep):
    pick(sizes, 0, inside, sep_rows, table, held, length, keep)


def pick(sizes, side, inside, sep_rows, table, held, length, out):
    _, rows, cols, lines = sizes
    for chip, lanes, block in spots(table, side, out.shape[0], length):
        out[chip, :, lanes] = held[block]
    if not inside:
        return
    wide = sep_rows // BLOCK
    me = lax.axis_index("col")
    plane = lax.axis_index("leaf") * lines + me // CORES
    for chip in range(out.shape[0]):
        other = plane ^ chip
        col = (other % lines) * CORES + core_of(me, side, chip)
        for row in range(rows):
            for w in range(wide):
                block = ((other // lines * rows + row) * cols + col) * wide + w
                at = length + (row * wide + w) * BLOCK
                out[chip, :, at : at + BLOCK] = held[block]


def pull_kernel(first, pulled, update, out):
    subs, up, _ = update.shape
    role = role_of(lax.axis_index("col"))
    for i in range(out.shape[0]):
        slot = first + i
        value = pulled[:, slot * up : (slot + 1) * up]
        matrix = update[sub_of(slot, subs // CORES, role)]
        out[i] = dot3(value, split(matrix), COLUMNS_OF)


def solve_kernel(mine, other, pull_mine, pull_other, inverse, out):
    half = mine.shape[0]
    role = role_of(lax.axis_index("col"))
    for slot in range(2 * half):
        if slot < half:
            value = mine[slot] - pull_mine[slot]
        else:
            value = other[slot - half] - pull_other[slot - half]
        sub = sub_of(slot, half, role)
        out[sub] = dot3(value, split(inverse[sub]), COLUMNS_OF)


def solve_parts_kernel(rows, masks, first, vectors, pull, own, inverse, *outs):
    half, width = vectors.shape[0], inverse.shape[2]
    share = width // rows
    sep_rows = own.shape[1] // rows
    row, role = lax.axis_index("row"), role_of(lax.axis_index("col"))
    for i in range(half):
        value = vectors[i] - pull[i]
        sub = sub_of(first + i, half, role)
        for mask, out in zip(masks, outs, strict=True):
            columns = pl.ds(pl.multiple_of((row ^ mask) * share, share), share)
            terms = dot3(value, split(inverse[sub, :, columns]), COLUMNS_OF)
            out[:, i * share : (i + 1) * share] = terms
    if first == 0:
        for mask, out in zip(masks, outs, strict=True):
            columns = pl.ds(pl.multiple_of((row ^ mask) * sep_rows, sep_rows), sep_rows)
            out[:, half * share :] = own[:, columns]


def finish_kernel(*refs):
    *parts, leaf_out, sep_out = refs
    subs, _, share = leaf_out.shape
    half, sep_rows = subs // CORES, sep_out.shape[1]
    role = role_of(lax.axis_index("col"))
    done = parts[0][...]
    for part in parts[1:]:
        done = done + part[...]
    for slot in range(subs):
        at = slot * share + (0 if slot < half else sep_rows)
        leaf_out[sub_of(slot, half, role)] = done[:, at : at + share]
    sep_out[...] = done[:, half * share : half * share + sep_rows]


def swap(value, axes, size, mask):
    return lax.ppermute(value, axes, [(i, i ^ mask) for i in range(size)])


def picked(value, dim, index, count):
    return jnp.stack(
        [lax.dynamic_index_in_dim(value, index ^ m, dim, keepdims=False) for m in range(count)], dim
    )


def beside(arrived, value):
    value = pl.pallas_call(
        load_kernel,
        out_shape=pltpu.VMEM(value.shape, value.dtype),
        in_specs=[HBM],
        out_specs=pl.BlockSpec(memory_space=pl.ANY),
        scratch_shapes=[pltpu.SemaphoreType.DMA((value.shape[0],))],
        compiler_params=pltpu.CompilerParams(vmem_limit_bytes=MIB),
        cost_estimate=pl.CostEstimate(flops=0, bytes_accessed=4 * value.size, transcendentals=0),
    )(in_hbm(value))
    return lax.optimization_barrier((arrived, value))


def sum_over_lines(mine, cols, arrived=None):
    step = CORES
    while step < cols:
        first = arrived is not None and step == CORES
        mine = mine + (arrived if first else swap(mine, "col", cols, step + 1))
        step *= 2
    return mine, swap(mine, "col", cols, 1)


def call(kernel, out_shape, in_specs, limit, cost, scratch=()):
    flops, nbytes = cost
    return pl.pallas_call(
        kernel,
        out_shape=out_shape,
        in_specs=in_specs,
        scratch_shapes=scratch,
        compiler_params=pltpu.CompilerParams(vmem_limit_bytes=limit * MIB),
        cost_estimate=pl.CostEstimate(flops=flops, bytes_accessed=nbytes, transcendentals=0),
    )


def body(sizes, leaf_rhs, leaf_inverse, update_rows, update_map, sep_rhs, sep_inverse):
    leaves, rows, cols = sizes
    lines = cols // CORES
    chips = leaves * lines
    subs, nrhs, _ = leaf_rhs.shape
    half = subs // CORES
    width = sep_rhs.shape[1]
    sep_rows = sep_inverse.shape[0]
    _, leaf_rows, leaf_cols = leaf_inverse.shape
    up = update_rows.shape[1]
    leaf, row, col = (lax.axis_index(a) for a in ("leaf", "row", "col"))
    core, line = col % CORES, col // CORES
    plane = leaf * lines + line
    plane_axes, plane_size = ("leaf", "col"), leaves * cols

    vec = jax.ShapeDtypeStruct((half, nrhs, leaf_rows), F32)
    leaf_flops = 2 * nrhs * leaf_inverse.size
    half_shape = (half, leaf_rows, leaf_cols)
    other, kept = pl.pallas_call(
        leaf_kernel,
        out_shape=[pltpu.VMEM(vec.shape, F32), pltpu.VMEM(half_shape, F32)],
        in_specs=[HBM, HBM],
        out_specs=[WHOLE, pl.BlockSpec(memory_space=pl.ANY)],
        scratch_shapes=[
            pltpu.VMEM(leaf_rhs.shape, F32),
            pltpu.VMEM(half_shape, F32),
            pltpu.SemaphoreType.DMA((subs * (leaf_rows // chunk_of(leaf_rows)),)),
            pltpu.SemaphoreType.DMA,
        ],
        compiler_params=pltpu.CompilerParams(vmem_limit_bytes=LIMIT * MIB),
        cost_estimate=pl.CostEstimate(
            flops=leaf_flops, bytes_accessed=4 * leaf_inverse.size, transcendentals=0
        ),
    )(in_hbm(leaf_rhs), in_hbm(leaf_inverse))
    arrived = swap(other, "col", cols, 1)
    mine = call(rest_kernel, vec, [WHOLE, WHOLE], 12, (leaf_flops // 2, 2 * leaf_inverse.size))(
        leaf_rhs, in_vmem(kept)
    )
    mine = mine + arrived
    arrived, update = beside(swap(mine, "col", cols, CORES + 1), update_rows)
    mine, other = sum_over_lines(mine, cols, arrived)
    coupled = [
        call(
            functools.partial(couple_kernel, first),
            jax.ShapeDtypeStruct((nrhs, half * up), F32),
            [WHOLE, WHOLE],
            12,
            (nrhs * update_rows.size, 2 * update_rows.size),
        )(vectors, in_vmem(update))
        for first, vectors in ((0, mine), (half, other))
    ]
    coupled = jnp.concatenate(coupled, 1)
    arrived = [swap(coupled, "row", rows, k) for k in range(1, rows)]
    inside = sep_rows % BLOCK == 0
    prepared = pl.pallas_call(
        functools.partial(prepare_kernel, inside),
        out_shape=[pltpu.VMEM((2 * sep_rows, width), BF16)]
        + ([pltpu.VMEM((width, 2 * sep_rows), BF16)] if inside else []),
        in_specs=[HBM],
        scratch_shapes=[pltpu.VMEM(sep_inverse.shape, F32), pltpu.SemaphoreType.DMA],
        compiler_params=pltpu.CompilerParams(vmem_limit_bytes=12 * MIB),
        cost_estimate=pl.CostEstimate(
            flops=0, bytes_accessed=8 * sep_inverse.size, transcendentals=0
        ),
    )(in_hbm(sep_inverse))
    arrived, prepared = lax.optimization_barrier((arrived, prepared))
    coupled = coupled + sum(arrived)
    numbers = jnp.pad(
        update_map.astype(F32), ((0, nrhs - subs), (0, BLOCK - update_map.shape[1]))
    )
    coupled = jnp.concatenate([coupled, numbers], 1)
    near = jnp.stack(
        [coupled] + [swap(coupled, plane_axes, plane_size, CORES * m + 1) for m in range(1, chips)]
    )
    far = swap(near, "col", cols, 1)

    shape = (leaves, rows, cols, lines)
    size = subs * up
    start, table = pl.pallas_call(
        functools.partial(scatter_kernel, lines),
        out_shape=[
            jax.ShapeDtypeStruct((width // BLOCK, nrhs, BLOCK), F32),
            pltpu.SMEM((CORES, chips * size // BLOCK), jnp.int32),
        ],
        in_specs=[WHOLE, WHOLE],
        out_specs=[WHOLE, SCALARS],
        scratch_shapes=[pltpu.SMEM((chips, subs, BLOCK), F32), pltpu.SemaphoreType.DMA((chips,))],
        compiler_params=pltpu.CompilerParams(vmem_limit_bytes=4 * MIB),
        cost_estimate=pl.CostEstimate(
            flops=2 * nrhs * width, bytes_accessed=12 * nrhs * width, transcendentals=0
        ),
    )(near, sep_rhs)
    table = pltpu.with_memory_space_constraint(table, pltpu.SMEM)
    own_width = rows * sep_rows
    length = size + (own_width if inside else 0)
    piece = jax.ShapeDtypeStruct((chips, nrhs, length), F32)
    send, held = call(
        functools.partial(separator_kernel, shape, inside),
        (piece, jax.ShapeDtypeStruct((width // BLOCK, nrhs, BLOCK), F32)),
        [SCALARS] + [WHOLE] * (2 + len(prepared)),
        12,
        (4 * nrhs * sep_inverse.size, 4 * sep_inverse.size),
    )(table, far, start, *map(in_vmem, prepared))
    keep = call(
        functools.partial(keep_kernel, shape, inside, sep_rows, size),
        piece,
        [SCALARS, WHOLE],
        4,
        (0, 8 * piece.size),
    )(table, held)
    if not inside:
        own = held.transpose(1, 0, 2).reshape(nrhs, leaves, rows, lines, CORES, sep_rows)
        own = own.transpose(4, 1, 3, 0, 2, 5).reshape(CORES, chips, nrhs, own_width)
        own = picked(picked(own, 0, core, CORES), 1, plane, chips)
        own = [jnp.concatenate([own[i][:1], own[1 - i][1:]]) for i in range(CORES)]
        keep = jnp.concatenate([keep, own[0]], 2)
        send = jnp.concatenate([send, own[1]], 2)
    keep = keep + swap(send, "col", cols, 1)
    pulled = keep[0] + sum(swap(keep[m], plane_axes, plane_size, CORES * m + 1) for m in range(1, chips))
    own = pulled[:, subs * up :]
    pulled = pulled[:, : subs * up]
    pulled = pulled + sum(swap(pulled, "row", rows, k) for k in range(1, rows))

    pull_other, pull_mine = (
        call(
            functools.partial(pull_kernel, first),
            vec,
            [WHOLE, WHOLE],
            12,
            (nrhs * update_rows.size, 2 * update_rows.size),
        )(pulled, update_rows)
        for first in (half, 0)
    )
    pull_mine = pull_mine + swap(pull_other, "col", cols, 1)
    pull_mine, pull_other = sum_over_lines(pull_mine, cols)
    share = leaf_cols // rows
    if inside and share % BLOCK == 0:
        def parts_of(masks):
            halves = [
                call(
                    functools.partial(solve_parts_kernel, rows, masks, first),
                    (jax.ShapeDtypeStruct((nrhs, half * share + (0 if first else sep_rows)), F32),)
                    * len(masks),
                    [WHOLE] * 4,
                    16,
                    (leaf_flops * len(masks) // (2 * rows), 2 * leaf_inverse.size * len(masks) // rows),
                )(vectors, pull, own, leaf_inverse)
                for first, vectors, pull in ((0, mine, pull_mine), (half, other, pull_other))
            ]
            return [jnp.concatenate(pair, 1) for pair in zip(*halves, strict=True)]

        far_parts = [swap(part, "row", rows, k) for k, part in enumerate(parts_of(tuple(range(1, rows))), 1)]
        parts = parts_of((0,)) + far_parts
        return call(
            finish_kernel,
            (
                jax.ShapeDtypeStruct((subs, nrhs, share), F32),
                jax.ShapeDtypeStruct((nrhs, sep_rows), F32),
            ),
            [WHOLE] * rows,
            4,
            (parts[0].size * rows, 4 * parts[0].size * rows),
        )(*parts)
    terms = call(
        solve_kernel,
        jax.ShapeDtypeStruct((subs, nrhs, leaf_cols), F32),
        [WHOLE] * 5,
        16,
        (leaf_flops, 4 * leaf_inverse.size),
    )(mine, other, pull_mine, pull_other, leaf_inverse)

    def last(k):
        leaf_part = lax.dynamic_slice_in_dim(terms, (row ^ k) * share, share, 2)
        own_part = lax.dynamic_slice_in_dim(own, (row ^ k) * sep_rows, sep_rows, 1)
        return jnp.concatenate([*leaf_part, own_part], 1)

    parts = [last(0)] + [swap(last(k), "row", rows, k) for k in range(1, rows)]
    done = sum(parts[1:]) + parts[0]
    leaf_solution = jnp.stack([done[:, s * share : (s + 1) * share] for s in range(subs)])
    return (leaf_solution, done[:, subs * share :])


def solution(mesh):
    sizes = tuple(mesh.shape[a] for a in ("leaf", "row", "col"))
    in_specs = (
        P("leaf", None, "col"),
        P("leaf", "row", "col"),
        P("leaf", "col", "row"),
        P("leaf", None),
        P(),
        P(("leaf", "row", "col"), None),
    )
    out_specs = (P("leaf", None, ("col", "row")), P(None, ("leaf", "row", "col")))
    return jax.shard_map(
        functools.partial(body, sizes), mesh=mesh, in_specs=in_specs, out_specs=out_specs, check_vma=False
    )
```

```python
import functools

import jax
import jax.numpy as jnp
from jax import lax
from jax.experimental import pallas as pl
from jax.experimental.pallas import tpu as pltpu
from jax.sharding import PartitionSpec as P

BLOCK = 128
CORES = 2
MIB = 1 << 20
LIMIT = 56

F32, BF16 = jnp.float32, jnp.bfloat16
HBM = pl.BlockSpec(memory_space=pltpu.HBM)
SCALARS = pl.BlockSpec(memory_space=pltpu.SMEM)
WHOLE = pl.BlockSpec(memory_space=pltpu.VMEM)


def in_hbm(value):
    return pltpu.with_memory_space_constraint(value, pltpu.HBM)


def in_vmem(value):
    return pltpu.with_memory_space_constraint(value, pltpu.VMEM)


def split(value):
    high = value.astype(BF16)
    return high, (value - high.astype(F32)).astype(BF16)


def dot3(value, halves, dims):
    rows = value.shape[0]
    high, low = halves
    parts = jnp.concatenate(split(value))
    main = lax.dot_general(parts, high, dims, preferred_element_type=F32)
    rest = lax.dot_general(parts[:rows], low, dims, preferred_element_type=F32)
    return main[:rows] + (main[rows:] + rest)


ROWS_OF = (((1,), (1,)), ((), ()))
COLUMNS_OF = (((1,), (0,)), ((), ()))


def role_of(col):
    for shift in (1, 2, 4, 8):
        col = col ^ (col >> shift)
    return col & 1


def sub_of(slot, half, role):
    return role * half + slot if slot < half else (1 - role) * half + (slot - half)


def chunk_of(rows):
    return min(rows // 2, 512)


def leaf_kernel(rhs, inverse, other, begun, kept, held, land, sems, rhs_sem):
    subs, rows, _ = land.shape
    half = subs // CORES
    role = role_of(lax.axis_index("col"))
    chunk = kept.shape[1]
    steps = rows // chunk

    def fetch(slot, step):
        part = pl.ds(step * chunk, chunk)
        last = slot < half and step == steps - 1
        return pltpu.make_async_copy(
            inverse.at[sub_of(slot, half, role), part],
            kept.at[slot] if last else land.at[slot, part],
            sems.at[slot * steps + step],
        )

    order = [(slot, step) for slot in range(half, subs) for step in range(steps)]
    order += [(slot, step) for step in range(steps) for slot in range(half)]
    first = pltpu.make_async_copy(rhs, held, rhs_sem)
    first.start()
    for slot, step in order:
        fetch(slot, step).start()
    first.wait()
    for slot, step in order:
        fetch(slot, step).wait()
        if slot < half and step == steps - 1:
            continue
        part = pl.ds(step * chunk, chunk)
        out, at = (begun, slot) if slot < half else (other, slot - half)
        value = held[sub_of(slot, half, role)]
        out[at, :, part] = dot3(value, split(land[slot, part]), ROWS_OF)


def rest_kernel(rhs, begun, kept, mine):
    half, chunk, _ = kept.shape
    done = begun.shape[2]
    role = role_of(lax.axis_index("col"))
    for slot in range(half):
        value = rhs[sub_of(slot, half, role)]
        mine[slot, :, :done] = begun[slot]
        mine[slot, :, done:] = dot3(value, split(kept[slot]), ROWS_OF)


def couple_kernel(first, vectors, update, out):
    subs, up, _ = update.shape
    role = role_of(lax.axis_index("col"))
    for i in range(vectors.shape[0]):
        matrix = update[sub_of(first + i, subs // CORES, role)]
        out[:, i * up : (i + 1) * up] = dot3(vectors[i], split(matrix), ROWS_OF)


def load_kernel(value, out, sems):
    count = sems.shape[0]
    step = value.shape[0] // count
    copies = [
        pltpu.make_async_copy(
            value.at[pl.ds(i * step, step)], out.at[pl.ds(i * step, step)], sems.at[i]
        )
        for i in range(count)
    ]
    for copy in copies:
        copy.start()
    for copy in copies:
        copy.wait()


def numbers_of(pieces, numbers, sems):
    _, subs, _ = numbers.shape
    at = pieces.shape[2] - BLOCK
    return [
        pltpu.make_async_copy(
            pieces.at[chip, pl.ds(0, subs), pl.ds(at, BLOCK)], numbers.at[chip], sems.at[chip]
        )
        for chip in range(pieces.shape[0])
    ]


def core_of(col, side, chip):
    return (col + side + (chip > 0)) % CORES


def spots(table, side, chips, length):
    count = length // BLOCK
    for chip in range(chips):
        for k in range(count):
            yield chip, slice(k * BLOCK, (k + 1) * BLOCK), table[side, chip * count + k]


def scatter_kernel(lines, near, rhs, out, table, numbers, sems):
    chips, _, length = near.shape
    length -= BLOCK
    subs = numbers.shape[1]
    here = length // (subs * BLOCK)
    me = lax.axis_index("col")
    copies = numbers_of(near, numbers, sems)
    for copy in copies:
        copy.start()
    for b in range(out.shape[0]):
        out[b] = rhs[:, b * BLOCK : (b + 1) * BLOCK]
    for copy in copies:
        copy.wait()
    for side in range(CORES):
        for chip in range(chips):
            col = (me // CORES ^ (chip % lines)) * CORES + core_of(me, side, chip)
            role = role_of(col)
            for slot in range(subs):
                sub = sub_of(slot, subs // CORES, role)
                for k in range(here):
                    block = numbers[chip, sub, col * here + k].astype(jnp.int32)
                    table[side, (chip * subs + slot) * here + k] = block
    for chip, lanes, block in spots(table, 0, chips, length):
        out[block] -= near[chip, :, lanes]


def prepare_kernel(inside, sep, both, *rest):
    *tall, land, sem = rest
    rows = sep.shape[0]
    copy = pltpu.make_async_copy(sep, land, sem)
    copy.start()
    copy.wait()
    both[:rows], both[rows:] = split(land[...])
    if inside:
        tall[0][:, :rows], tall[0][:, rows:] = split(land[...].T)


def separator_kernel(sizes, inside, table, far, start, both, *rest):
    *tall, send, held = rest
    chips, nrhs, length = far.shape
    length -= BLOCK
    total = held.shape[0]
    sep_rows = both.shape[0] // 2

    held[...] = start[...]
    for chip, lanes, block in spots(table, 1, chips, length):
        held[block] -= far[chip, :, lanes]
    updated = jnp.concatenate(split(jnp.concatenate([held[b] for b in range(total)], 1)))
    matrix, dims = (tall[0], COLUMNS_OF) if inside else (both, ROWS_OF)
    forward = lax.dot_general(updated, matrix[...], dims, preferred_element_type=F32)
    forward = forward[:nrhs, :sep_rows] + (forward[nrhs:, :sep_rows] + forward[:nrhs, sep_rows:])
    high, low = split(forward)
    parts = jnp.concatenate(
        [jnp.concatenate([high, high], 1), jnp.concatenate([low, jnp.zeros_like(low)], 1)]
    )
    terms = lax.dot_general(parts, both[...], COLUMNS_OF, preferred_element_type=F32)
    terms = terms[:nrhs] + terms[nrhs:]
    for b in range(total):
        held[b] = terms[:, b * BLOCK : (b + 1) * BLOCK]
    pick(sizes, 1, inside, sep_rows, table, held, length, send)


def keep_kernel(sizes, inside, sep_rows, length, table, held, keep):
    pick(sizes, 0, inside, sep_rows, table, held, length, keep)


def pick(sizes, side, inside, sep_rows, table, held, length, out):
    _, rows, cols, lines = sizes
    for chip, lanes, block in spots(table, side, out.shape[0], length):
        out[chip, :, lanes] = held[block]
    if not inside:
        return
    wide = sep_rows // BLOCK
    me = lax.axis_index("col")
    plane = lax.axis_index("leaf") * lines + me // CORES
    for chip in range(out.shape[0]):
        other = plane ^ chip
        col = (other % lines) * CORES + core_of(me, side, chip)
        for row in range(rows):
            for w in range(wide):
                block = ((other // lines * rows + row) * cols + col) * wide + w
                at = length + (row * wide + w) * BLOCK
                out[chip, :, at : at + BLOCK] = held[block]


def pull_kernel(first, pulled, update, out):
    subs, up, _ = update.shape
    role = role_of(lax.axis_index("col"))
    for i in range(out.shape[0]):
        slot = first + i
        value = pulled[:, slot * up : (slot + 1) * up]
        matrix = update[sub_of(slot, subs // CORES, role)]
        out[i] = dot3(value, split(matrix), COLUMNS_OF)


def solve_kernel(mine, other, pull_mine, pull_other, inverse, out):
    half = mine.shape[0]
    role = role_of(lax.axis_index("col"))
    for slot in range(2 * half):
        if slot < half:
            value = mine[slot] - pull_mine[slot]
        else:
            value = other[slot - half] - pull_other[slot - half]
        sub = sub_of(slot, half, role)
        out[sub] = dot3(value, split(inverse[sub]), COLUMNS_OF)


def solve_parts_kernel(rows, masks, first, vectors, pull, own, inverse, *outs):
    half, width = vectors.shape[0], inverse.shape[2]
    share = width // rows
    sep_rows = own.shape[1] // rows
    row, role = lax.axis_index("row"), role_of(lax.axis_index("col"))
    for i in range(half):
        value = vectors[i] - pull[i]
        sub = sub_of(first + i, half, role)
        for mask, out in zip(masks, outs, strict=True):
            columns = pl.ds(pl.multiple_of((row ^ mask) * share, share), share)
            terms = dot3(value, split(inverse[sub, :, columns]), COLUMNS_OF)
            out[:, i * share : (i + 1) * share] = terms
    if first == 0:
        for mask, out in zip(masks, outs, strict=True):
            columns = pl.ds(pl.multiple_of((row ^ mask) * sep_rows, sep_rows), sep_rows)
            out[:, half * share :] = own[:, columns]


def finish_kernel(*refs):
    *parts, leaf_out, sep_out = refs
    subs, _, share = leaf_out.shape
    half, sep_rows = subs // CORES, sep_out.shape[1]
    role = role_of(lax.axis_index("col"))
    done = parts[0][...]
    for part in parts[1:]:
        done = done + part[...]
    for slot in range(subs):
        at = slot * share + (0 if slot < half else sep_rows)
        leaf_out[sub_of(slot, half, role)] = done[:, at : at + share]
    sep_out[...] = done[:, half * share : half * share + sep_rows]


def swap(value, axes, size, mask):
    return lax.ppermute(value, axes, [(i, i ^ mask) for i in range(size)])


def picked(value, dim, index, count):
    return jnp.stack(
        [lax.dynamic_index_in_dim(value, index ^ m, dim, keepdims=False) for m in range(count)], dim
    )


def beside(arrived, value):
    value = pl.pallas_call(
        load_kernel,
        out_shape=pltpu.VMEM(value.shape, value.dtype),
        in_specs=[HBM],
        out_specs=pl.BlockSpec(memory_space=pl.ANY),
        scratch_shapes=[pltpu.SemaphoreType.DMA((value.shape[0],))],
        compiler_params=pltpu.CompilerParams(vmem_limit_bytes=MIB),
        cost_estimate=pl.CostEstimate(flops=0, bytes_accessed=4 * value.size, transcendentals=0),
    )(in_hbm(value))
    return lax.optimization_barrier((arrived, value))


def sum_over_lines(mine, cols, arrived=None):
    step = CORES
    while step < cols:
        first = arrived is not None and step == CORES
        mine = mine + (arrived if first else swap(mine, "col", cols, step + 1))
        step *= 2
    return mine, swap(mine, "col", cols, 1)


def call(kernel, out_shape, in_specs, limit, cost, scratch=()):
    flops, nbytes = cost
    return pl.pallas_call(
        kernel,
        out_shape=out_shape,
        in_specs=in_specs,
        scratch_shapes=scratch,
        compiler_params=pltpu.CompilerParams(vmem_limit_bytes=limit * MIB),
        cost_estimate=pl.CostEstimate(flops=flops, bytes_accessed=nbytes, transcendentals=0),
    )


def body(sizes, leaf_rhs, leaf_inverse, update_rows, update_map, sep_rhs, sep_inverse):
    leaves, rows, cols = sizes
    lines = cols // CORES
    chips = leaves * lines
    subs, nrhs, _ = leaf_rhs.shape
    half = subs // CORES
    width = sep_rhs.shape[1]
    sep_rows = sep_inverse.shape[0]
    _, leaf_rows, leaf_cols = leaf_inverse.shape
    up = update_rows.shape[1]
    leaf, row, col = (lax.axis_index(a) for a in ("leaf", "row", "col"))
    core, line = col % CORES, col // CORES
    plane = leaf * lines + line
    plane_axes, plane_size = ("leaf", "col"), leaves * cols

    vec = jax.ShapeDtypeStruct((half, nrhs, leaf_rows), F32)
    leaf_flops = 2 * nrhs * leaf_inverse.size
    chunk = chunk_of(leaf_rows)
    other, begun, kept = pl.pallas_call(
        leaf_kernel,
        out_shape=[
            pltpu.VMEM(vec.shape, F32),
            pltpu.VMEM((half, nrhs, leaf_rows - chunk), F32),
            pltpu.VMEM((half, chunk, leaf_cols), F32),
        ],
        in_specs=[HBM, HBM],
        out_specs=[WHOLE, WHOLE, pl.BlockSpec(memory_space=pl.ANY)],
        scratch_shapes=[
            pltpu.VMEM(leaf_rhs.shape, F32),
            pltpu.VMEM(leaf_inverse.shape, F32),
            pltpu.SemaphoreType.DMA((subs * (leaf_rows // chunk),)),
            pltpu.SemaphoreType.DMA,
        ],
        compiler_params=pltpu.CompilerParams(vmem_limit_bytes=LIMIT * MIB),
        cost_estimate=pl.CostEstimate(
            flops=leaf_flops, bytes_accessed=4 * leaf_inverse.size, transcendentals=0
        ),
    )(in_hbm(leaf_rhs), in_hbm(leaf_inverse))
    arrived = swap(other, "col", cols, 1)
    mine = call(rest_kernel, vec, [WHOLE] * 3, 12, (leaf_flops // 4, leaf_inverse.size))(
        leaf_rhs, begun, in_vmem(kept)
    )
    mine = mine + arrived
    arrived, update = beside(swap(mine, "col", cols, CORES + 1), update_rows)
    mine, other = sum_over_lines(mine, cols, arrived)
    coupled = [
        call(
            functools.partial(couple_kernel, first),
            jax.ShapeDtypeStruct((nrhs, half * up), F32),
            [WHOLE, WHOLE],
            12,
            (nrhs * update_rows.size, 2 * update_rows.size),
        )(vectors, in_vmem(update))
        for first, vectors in ((0, mine), (half, other))
    ]
    coupled = jnp.concatenate(coupled, 1)
    arrived = [swap(coupled, "row", rows, k) for k in reversed(range(1, rows))]
    inside = sep_rows % BLOCK == 0
    prepared = pl.pallas_call(
        functools.partial(prepare_kernel, inside),
        out_shape=[pltpu.VMEM((2 * sep_rows, width), BF16)]
        + ([pltpu.VMEM((width, 2 * sep_rows), BF16)] if inside else []),
        in_specs=[HBM],
        scratch_shapes=[pltpu.VMEM(sep_inverse.shape, F32), pltpu.SemaphoreType.DMA],
        compiler_params=pltpu.CompilerParams(vmem_limit_bytes=12 * MIB),
        cost_estimate=pl.CostEstimate(
            flops=0, bytes_accessed=8 * sep_inverse.size, transcendentals=0
        ),
    )(in_hbm(sep_inverse))
    arrived, prepared = lax.optimization_barrier((arrived, prepared))
    coupled = coupled + sum(arrived)
    numbers = jnp.pad(
        update_map.astype(F32), ((0, nrhs - subs), (0, BLOCK - update_map.shape[1]))
    )
    coupled = jnp.concatenate([coupled, numbers], 1)
    near = jnp.stack(
        [coupled] + [swap(coupled, plane_axes, plane_size, CORES * m + 1) for m in range(1, chips)]
    )
    far = swap(near, "col", cols, 1)

    shape = (leaves, rows, cols, lines)
    size = subs * up
    start, table = pl.pallas_call(
        functools.partial(scatter_kernel, lines),
        out_shape=[
            jax.ShapeDtypeStruct((width // BLOCK, nrhs, BLOCK), F32),
            pltpu.SMEM((CORES, chips * size // BLOCK), jnp.int32),
        ],
        in_specs=[WHOLE, WHOLE],
        out_specs=[WHOLE, SCALARS],
        scratch_shapes=[pltpu.SMEM((chips, subs, BLOCK), F32), pltpu.SemaphoreType.DMA((chips,))],
        compiler_params=pltpu.CompilerParams(vmem_limit_bytes=4 * MIB),
        cost_estimate=pl.CostEstimate(
            flops=2 * nrhs * width, bytes_accessed=12 * nrhs * width, transcendentals=0
        ),
    )(near, sep_rhs)
    table = pltpu.with_memory_space_constraint(table, pltpu.SMEM)
    own_width = rows * sep_rows
    length = size + (own_width if inside else 0)
    piece = jax.ShapeDtypeStruct((chips, nrhs, length), F32)
    send, held = call(
        functools.partial(separator_kernel, shape, inside),
        (piece, jax.ShapeDtypeStruct((width // BLOCK, nrhs, BLOCK), F32)),
        [SCALARS] + [WHOLE] * (2 + len(prepared)),
        12,
        (4 * nrhs * sep_inverse.size, 4 * sep_inverse.size),
    )(table, far, start, *map(in_vmem, prepared))
    keep = call(
        functools.partial(keep_kernel, shape, inside, sep_rows, size),
        piece,
        [SCALARS, WHOLE],
        4,
        (0, 8 * piece.size),
    )(table, held)
    if not inside:
        own = held.transpose(1, 0, 2).reshape(nrhs, leaves, rows, lines, CORES, sep_rows)
        own = own.transpose(4, 1, 3, 0, 2, 5).reshape(CORES, chips, nrhs, own_width)
        own = picked(picked(own, 0, core, CORES), 1, plane, chips)
        own = [jnp.concatenate([own[i][:1], own[1 - i][1:]]) for i in range(CORES)]
        keep = jnp.concatenate([keep, own[0]], 2)
        send = jnp.concatenate([send, own[1]], 2)
    keep = keep + swap(send, "col", cols, 1)
    pulled = keep[0] + sum(swap(keep[m], plane_axes, plane_size, CORES * m + 1) for m in reversed(range(1, chips)))
    own = pulled[:, subs * up :]
    pulled = pulled[:, : subs * up]
    pulled = pulled + sum(swap(pulled, "row", rows, k) for k in reversed(range(1, rows)))

    pull_other, pull_mine = (
        call(
            functools.partial(pull_kernel, first),
            vec,
            [WHOLE, WHOLE],
            12,
            (nrhs * update_rows.size, 2 * update_rows.size),
        )(pulled, update_rows)
        for first in (half, 0)
    )
    pull_mine = pull_mine + swap(pull_other, "col", cols, 1)
    pull_mine, pull_other = sum_over_lines(pull_mine, cols)
    share = leaf_cols // rows
    if inside and share % BLOCK == 0:
        def parts_of(masks):
            halves = [
                call(
                    functools.partial(solve_parts_kernel, rows, masks, first),
                    (jax.ShapeDtypeStruct((nrhs, half * share + (0 if first else sep_rows)), F32),)
                    * len(masks),
                    [WHOLE] * 4,
                    16,
                    (leaf_flops * len(masks) // (2 * rows), 2 * leaf_inverse.size * len(masks) // rows),
                )(vectors, pull, own, leaf_inverse)
                for first, vectors, pull in ((0, mine, pull_mine), (half, other, pull_other))
            ]
            return [jnp.concatenate(pair, 1) for pair in zip(*halves, strict=True)]

        far_parts = [swap(part, "row", rows, k) for k, part in enumerate(parts_of(tuple(range(1, rows))), 1)]
        parts = parts_of((0,)) + far_parts
        return call(
            finish_kernel,
            (
                jax.ShapeDtypeStruct((subs, nrhs, share), F32),
                jax.ShapeDtypeStruct((nrhs, sep_rows), F32),
            ),
            [WHOLE] * rows,
            4,
            (parts[0].size * rows, 4 * parts[0].size * rows),
        )(*parts)
    terms = call(
        solve_kernel,
        jax.ShapeDtypeStruct((subs, nrhs, leaf_cols), F32),
        [WHOLE] * 5,
        16,
        (leaf_flops, 4 * leaf_inverse.size),
    )(mine, other, pull_mine, pull_other, leaf_inverse)

    def last(k):
        leaf_part = lax.dynamic_slice_in_dim(terms, (row ^ k) * share, share, 2)
        own_part = lax.dynamic_slice_in_dim(own, (row ^ k) * sep_rows, sep_rows, 1)
        return jnp.concatenate([*leaf_part, own_part], 1)

    parts = [last(0)] + [swap(last(k), "row", rows, k) for k in range(1, rows)]
    done = sum(parts[1:]) + parts[0]
    leaf_solution = jnp.stack([done[:, s * share : (s + 1) * share] for s in range(subs)])
    return (leaf_solution, done[:, subs * share :])


def solution(mesh):
    sizes = tuple(mesh.shape[a] for a in ("leaf", "row", "col"))
    in_specs = (
        P("leaf", None, "col"),
        P("leaf", "row", "col"),
        P("leaf", "col", "row"),
        P("leaf", None),
        P(),
        P(("leaf", "row", "col"), None),
    )
    out_specs = (P("leaf", None, ("col", "row")), P(None, ("leaf", "row", "col")))
    return jax.shard_map(
        functools.partial(body, sizes), mesh=mesh, in_specs=in_specs, out_specs=out_specs, check_vma=False
    )
```

```python
import functools

import jax
import jax.numpy as jnp
from jax import lax
from jax.experimental import pallas as pl
from jax.experimental.pallas import tpu as pltpu
from jax.sharding import PartitionSpec as P

BLOCK = 128
CORES = 2
MIB = 1 << 20
LIMIT = 56

F32, BF16 = jnp.float32, jnp.bfloat16
HBM = pl.BlockSpec(memory_space=pltpu.HBM)
SCALARS = pl.BlockSpec(memory_space=pltpu.SMEM)
WHOLE = pl.BlockSpec(memory_space=pltpu.VMEM)


def in_hbm(value):
    return pltpu.with_memory_space_constraint(value, pltpu.HBM)


def in_vmem(value):
    return pltpu.with_memory_space_constraint(value, pltpu.VMEM)


def split(value):
    high = value.astype(BF16)
    return high, (value - high.astype(F32)).astype(BF16)


def dot3(value, halves, dims):
    rows = value.shape[0]
    high, low = halves
    parts = jnp.concatenate(split(value))
    main = lax.dot_general(parts, high, dims, preferred_element_type=F32)
    rest = lax.dot_general(parts[:rows], low, dims, preferred_element_type=F32)
    return main[:rows] + (main[rows:] + rest)


ROWS_OF = (((1,), (1,)), ((), ()))
COLUMNS_OF = (((1,), (0,)), ((), ()))


def role_of(col):
    for shift in (1, 2, 4, 8):
        col = col ^ (col >> shift)
    return col & 1


def sub_of(slot, half, role):
    return role * half + slot if slot < half else (1 - role) * half + (slot - half)


def chunk_of(rows):
    return min(rows // 2, 512)


def leaf_kernel(rhs, inverse, other, begun, kept, held, land, sems, rhs_sem):
    subs, rows, _ = land.shape
    half = subs // CORES
    role = role_of(lax.axis_index("col"))
    chunk = kept.shape[1]
    steps = rows // chunk

    def fetch(slot, step):
        part = pl.ds(step * chunk, chunk)
        last = slot < half and step == steps - 1
        return pltpu.make_async_copy(
            inverse.at[sub_of(slot, half, role), part],
            kept.at[slot] if last else land.at[slot, part],
            sems.at[slot * steps + step],
        )

    order = [(slot, step) for slot in range(half, subs) for step in range(steps)]
    order += [(slot, step) for step in range(steps) for slot in range(half)]
    first = pltpu.make_async_copy(rhs, held, rhs_sem)
    first.start()
    for slot, step in order:
        fetch(slot, step).start()
    first.wait()
    for slot, step in order:
        fetch(slot, step).wait()
        if slot < half and step == steps - 1:
            continue
        part = pl.ds(step * chunk, chunk)
        out, at = (begun, slot) if slot < half else (other, slot - half)
        value = held[sub_of(slot, half, role)]
        out[at, :, part] = dot3(value, split(land[slot, part]), ROWS_OF)


def rest_kernel(rhs, begun, kept, mine):
    half, chunk, _ = kept.shape
    done = begun.shape[2]
    role = role_of(lax.axis_index("col"))
    for slot in range(half):
        value = rhs[sub_of(slot, half, role)]
        mine[slot, :, :done] = begun[slot]
        mine[slot, :, done:] = dot3(value, split(kept[slot]), ROWS_OF)


def couple_kernel(first, vectors, update, out):
    subs, up, _ = update.shape
    role = role_of(lax.axis_index("col"))
    for i in range(vectors.shape[0]):
        matrix = update[sub_of(first + i, subs // CORES, role)]
        out[:, i * up : (i + 1) * up] = dot3(vectors[i], split(matrix), ROWS_OF)


def load_kernel(value, out, sems):
    count = sems.shape[0]
    step = value.shape[0] // count
    copies = [
        pltpu.make_async_copy(
            value.at[pl.ds(i * step, step)], out.at[pl.ds(i * step, step)], sems.at[i]
        )
        for i in range(count)
    ]
    for copy in copies:
        copy.start()
    for copy in copies:
        copy.wait()


def numbers_of(pieces, numbers, sems):
    _, subs, _ = numbers.shape
    at = pieces.shape[2] - BLOCK
    return [
        pltpu.make_async_copy(
            pieces.at[chip, pl.ds(0, subs), pl.ds(at, BLOCK)], numbers.at[chip], sems.at[chip]
        )
        for chip in range(pieces.shape[0])
    ]


def core_of(col, side, chip):
    return (col + side + (chip > 0)) % CORES


def spots(table, side, chips, length):
    count = length // BLOCK
    for chip in range(chips):
        for k in range(count):
            yield chip, slice(k * BLOCK, (k + 1) * BLOCK), table[side, chip * count + k]


def scatter_kernel(lines, near, rhs, out, table, numbers, sems):
    chips, _, length = near.shape
    length -= BLOCK
    subs = numbers.shape[1]
    here = length // (subs * BLOCK)
    me = lax.axis_index("col")
    copies = numbers_of(near, numbers, sems)
    for copy in copies:
        copy.start()
    for b in range(out.shape[0]):
        out[b] = rhs[:, b * BLOCK : (b + 1) * BLOCK]
    for copy in copies:
        copy.wait()
    for side in range(CORES):
        for chip in range(chips):
            col = (me // CORES ^ (chip % lines)) * CORES + core_of(me, side, chip)
            role = role_of(col)
            for slot in range(subs):
                sub = sub_of(slot, subs // CORES, role)
                for k in range(here):
                    block = numbers[chip, sub, col * here + k].astype(jnp.int32)
                    table[side, (chip * subs + slot) * here + k] = block
    for chip, lanes, block in spots(table, 0, chips, length):
        out[block] -= near[chip, :, lanes]


def prepare_kernel(inside, sep, both, *rest):
    *tall, land, sem = rest
    rows = sep.shape[0]
    copy = pltpu.make_async_copy(sep, land, sem)
    copy.start()
    copy.wait()
    both[:rows], both[rows:] = split(land[...])
    if inside:
        tall[0][:, :rows], tall[0][:, rows:] = split(land[...].T)


def separator_kernel(sizes, inside, table, far, start, both, *rest):
    *tall, send, held = rest
    chips, nrhs, length = far.shape
    length -= BLOCK
    total = held.shape[0]
    sep_rows = both.shape[0] // 2

    held[...] = start[...]
    for chip, lanes, block in spots(table, 1, chips, length):
        held[block] -= far[chip, :, lanes]
    updated = jnp.concatenate(split(jnp.concatenate([held[b] for b in range(total)], 1)))
    matrix, dims = (tall[0], COLUMNS_OF) if inside else (both, ROWS_OF)
    forward = lax.dot_general(updated, matrix[...], dims, preferred_element_type=F32)
    forward = forward[:nrhs, :sep_rows] + (forward[nrhs:, :sep_rows] + forward[:nrhs, sep_rows:])
    high, low = split(forward)
    parts = jnp.concatenate(
        [jnp.concatenate([high, high], 1), jnp.concatenate([low, jnp.zeros_like(low)], 1)]
    )
    terms = lax.dot_general(parts, both[...], COLUMNS_OF, preferred_element_type=F32)
    terms = terms[:nrhs] + terms[nrhs:]
    for b in range(total):
        held[b] = terms[:, b * BLOCK : (b + 1) * BLOCK]
    pick(sizes, 1, inside, sep_rows, table, held, length, send)


def keep_kernel(sizes, inside, sep_rows, length, table, held, keep):
    pick(sizes, 0, inside, sep_rows, table, held, length, keep)


def pick(sizes, side, inside, sep_rows, table, held, length, out):
    _, rows, cols, lines = sizes
    for chip, lanes, block in spots(table, side, out.shape[0], length):
        out[chip, :, lanes] = held[block]
    if not inside:
        return
    wide = sep_rows // BLOCK
    me = lax.axis_index("col")
    plane = lax.axis_index("leaf") * lines + me // CORES
    for chip in range(out.shape[0]):
        other = plane ^ chip
        col = (other % lines) * CORES + core_of(me, side, chip)
        for row in range(rows):
            for w in range(wide):
                block = ((other // lines * rows + row) * cols + col) * wide + w
                at = length + (row * wide + w) * BLOCK
                out[chip, :, at : at + BLOCK] = held[block]


def pull_kernel(first, pulled, update, out):
    subs, up, _ = update.shape
    role = role_of(lax.axis_index("col"))
    for i in range(out.shape[0]):
        slot = first + i
        value = pulled[:, slot * up : (slot + 1) * up]
        matrix = update[sub_of(slot, subs // CORES, role)]
        out[i] = dot3(value, split(matrix), COLUMNS_OF)


def solve_kernel(mine, other, pull_mine, pull_other, inverse, out):
    half = mine.shape[0]
    role = role_of(lax.axis_index("col"))
    for slot in range(2 * half):
        if slot < half:
            value = mine[slot] - pull_mine[slot]
        else:
            value = other[slot - half] - pull_other[slot - half]
        sub = sub_of(slot, half, role)
        out[sub] = dot3(value, split(inverse[sub]), COLUMNS_OF)


def solve_parts_kernel(rows, masks, first, vectors, pull, own, inverse, *outs):
    half, width = vectors.shape[0], inverse.shape[2]
    share = width // rows
    sep_rows = own.shape[1] // rows
    row, role = lax.axis_index("row"), role_of(lax.axis_index("col"))
    for i in range(half):
        value = vectors[i] - pull[i]
        sub = sub_of(first + i, half, role)
        for mask, out in zip(masks, outs, strict=True):
            columns = pl.ds(pl.multiple_of((row ^ mask) * share, share), share)
            terms = dot3(value, split(inverse[sub, :, columns]), COLUMNS_OF)
            out[:, i * share : (i + 1) * share] = terms
    if first == 0:
        for mask, out in zip(masks, outs, strict=True):
            columns = pl.ds(pl.multiple_of((row ^ mask) * sep_rows, sep_rows), sep_rows)
            out[:, half * share :] = own[:, columns]


def finish_kernel(*refs):
    *parts, leaf_out, sep_out = refs
    subs, _, share = leaf_out.shape
    half, sep_rows = subs // CORES, sep_out.shape[1]
    role = role_of(lax.axis_index("col"))
    done = parts[0][...]
    for part in parts[1:]:
        done = done + part[...]
    for slot in range(subs):
        at = slot * share + (0 if slot < half else sep_rows)
        leaf_out[sub_of(slot, half, role)] = done[:, at : at + share]
    sep_out[...] = done[:, half * share : half * share + sep_rows]


def swap(value, axes, size, mask):
    return lax.ppermute(value, axes, [(i, i ^ mask) for i in range(size)])


def picked(value, dim, index, count):
    return jnp.stack(
        [lax.dynamic_index_in_dim(value, index ^ m, dim, keepdims=False) for m in range(count)], dim
    )


def beside(arrived, value):
    value = pl.pallas_call(
        load_kernel,
        out_shape=pltpu.VMEM(value.shape, value.dtype),
        in_specs=[HBM],
        out_specs=pl.BlockSpec(memory_space=pl.ANY),
        scratch_shapes=[pltpu.SemaphoreType.DMA((value.shape[0],))],
        compiler_params=pltpu.CompilerParams(vmem_limit_bytes=MIB),
        cost_estimate=pl.CostEstimate(flops=0, bytes_accessed=4 * value.size, transcendentals=0),
    )(in_hbm(value))
    return lax.optimization_barrier((arrived, value))


def sum_over_lines(mine, cols, arrived=None):
    step = CORES
    while step < cols:
        first = arrived is not None and step == CORES
        mine = mine + (arrived if first else swap(mine, "col", cols, step + 1))
        step *= 2
    return mine, swap(mine, "col", cols, 1)


def call(kernel, out_shape, in_specs, limit, cost, scratch=()):
    flops, nbytes = cost
    return pl.pallas_call(
        kernel,
        out_shape=out_shape,
        in_specs=in_specs,
        scratch_shapes=scratch,
        compiler_params=pltpu.CompilerParams(vmem_limit_bytes=limit * MIB),
        cost_estimate=pl.CostEstimate(flops=flops, bytes_accessed=nbytes, transcendentals=0),
    )


def body(sizes, leaf_rhs, leaf_inverse, update_rows, update_map, sep_rhs, sep_inverse):
    leaves, rows, cols = sizes
    lines = cols // CORES
    chips = leaves * lines
    subs, nrhs, _ = leaf_rhs.shape
    half = subs // CORES
    width = sep_rhs.shape[1]
    sep_rows = sep_inverse.shape[0]
    _, leaf_rows, leaf_cols = leaf_inverse.shape
    up = update_rows.shape[1]
    leaf, row, col = (lax.axis_index(a) for a in ("leaf", "row", "col"))
    core, line = col % CORES, col // CORES
    plane = leaf * lines + line
    plane_axes, plane_size = ("leaf", "col"), leaves * cols

    vec = jax.ShapeDtypeStruct((half, nrhs, leaf_rows), F32)
    leaf_flops = 2 * nrhs * leaf_inverse.size
    chunk = chunk_of(leaf_rows)
    other, begun, kept = pl.pallas_call(
        leaf_kernel,
        out_shape=[
            pltpu.VMEM(vec.shape, F32),
            pltpu.VMEM((half, nrhs, leaf_rows - chunk), F32),
            pltpu.VMEM((half, chunk, leaf_cols), F32),
        ],
        in_specs=[HBM, HBM],
        out_specs=[WHOLE, WHOLE, pl.BlockSpec(memory_space=pl.ANY)],
        scratch_shapes=[
            pltpu.VMEM(leaf_rhs.shape, F32),
            pltpu.VMEM(leaf_inverse.shape, F32),
            pltpu.SemaphoreType.DMA((subs * (leaf_rows // chunk),)),
            pltpu.SemaphoreType.DMA,
        ],
        compiler_params=pltpu.CompilerParams(vmem_limit_bytes=LIMIT * MIB),
        cost_estimate=pl.CostEstimate(
            flops=leaf_flops, bytes_accessed=4 * leaf_inverse.size, transcendentals=0
        ),
    )(in_hbm(leaf_rhs), in_hbm(leaf_inverse))
    arrived = swap(other, "col", cols, 1)
    mine = call(rest_kernel, vec, [WHOLE] * 3, 12, (leaf_flops // 4, leaf_inverse.size))(
        leaf_rhs, begun, in_vmem(kept)
    )
    mine = mine + arrived
    arrived, update = beside(swap(mine, "col", cols, CORES + 1), update_rows)
    mine, other = sum_over_lines(mine, cols, arrived)
    coupled = [
        call(
            functools.partial(couple_kernel, first),
            jax.ShapeDtypeStruct((nrhs, half * up), F32),
            [WHOLE, WHOLE],
            12,
            (nrhs * update_rows.size, 2 * update_rows.size),
        )(vectors, in_vmem(update))
        for first, vectors in ((0, mine), (half, other))
    ]
    coupled = jnp.concatenate(coupled, 1)
    arrived = [swap(coupled, "row", rows, k) for k in reversed(range(1, rows))]
    inside = sep_rows % BLOCK == 0
    prepared = pl.pallas_call(
        functools.partial(prepare_kernel, inside),
        out_shape=[pltpu.VMEM((2 * sep_rows, width), BF16)]
        + ([pltpu.VMEM((width, 2 * sep_rows), BF16)] if inside else []),
        in_specs=[HBM],
        scratch_shapes=[pltpu.VMEM(sep_inverse.shape, F32), pltpu.SemaphoreType.DMA],
        compiler_params=pltpu.CompilerParams(vmem_limit_bytes=12 * MIB),
        cost_estimate=pl.CostEstimate(
            flops=0, bytes_accessed=8 * sep_inverse.size, transcendentals=0
        ),
    )(in_hbm(sep_inverse))
    arrived, prepared = lax.optimization_barrier((arrived, prepared))
    coupled = coupled + sum(arrived)
    numbers = jnp.pad(
        update_map.astype(F32), ((0, nrhs - subs), (0, BLOCK - update_map.shape[1]))
    )
    coupled = jnp.concatenate([coupled, numbers], 1)
    near = jnp.stack(
        [coupled]
        + [swap(coupled, plane_axes, plane_size, CORES * m + 1) for m in reversed(range(1, chips))][::-1]
    )
    far = swap(near, "col", cols, 1)

    shape = (leaves, rows, cols, lines)
    size = subs * up
    start, table = pl.pallas_call(
        functools.partial(scatter_kernel, lines),
        out_shape=[
            jax.ShapeDtypeStruct((width // BLOCK, nrhs, BLOCK), F32),
            pltpu.SMEM((CORES, chips * size // BLOCK), jnp.int32),
        ],
        in_specs=[WHOLE, WHOLE],
        out_specs=[WHOLE, SCALARS],
        scratch_shapes=[pltpu.SMEM((chips, subs, BLOCK), F32), pltpu.SemaphoreType.DMA((chips,))],
        compiler_params=pltpu.CompilerParams(vmem_limit_bytes=4 * MIB),
        cost_estimate=pl.CostEstimate(
            flops=2 * nrhs * width, bytes_accessed=12 * nrhs * width, transcendentals=0
        ),
    )(near, sep_rhs)
    table = pltpu.with_memory_space_constraint(table, pltpu.SMEM)
    own_width = rows * sep_rows
    length = size + (own_width if inside else 0)
    piece = jax.ShapeDtypeStruct((chips, nrhs, length), F32)
    send, held = call(
        functools.partial(separator_kernel, shape, inside),
        (piece, jax.ShapeDtypeStruct((width // BLOCK, nrhs, BLOCK), F32)),
        [SCALARS] + [WHOLE] * (2 + len(prepared)),
        12,
        (4 * nrhs * sep_inverse.size, 4 * sep_inverse.size),
    )(table, far, start, *map(in_vmem, prepared))
    keep = call(
        functools.partial(keep_kernel, shape, inside, sep_rows, size),
        piece,
        [SCALARS, WHOLE],
        4,
        (0, 8 * piece.size),
    )(table, held)
    if not inside:
        own = held.transpose(1, 0, 2).reshape(nrhs, leaves, rows, lines, CORES, sep_rows)
        own = own.transpose(4, 1, 3, 0, 2, 5).reshape(CORES, chips, nrhs, own_width)
        own = picked(picked(own, 0, core, CORES), 1, plane, chips)
        own = [jnp.concatenate([own[i][:1], own[1 - i][1:]]) for i in range(CORES)]
        keep = jnp.concatenate([keep, own[0]], 2)
        send = jnp.concatenate([send, own[1]], 2)
    keep = keep + swap(send, "col", cols, 1)
    pulled = keep[0] + sum(swap(keep[m], plane_axes, plane_size, CORES * m + 1) for m in reversed(range(1, chips)))
    own = pulled[:, subs * up :]
    pulled = pulled[:, : subs * up]
    pulled = pulled + sum(swap(pulled, "row", rows, k) for k in reversed(range(1, rows)))

    pull_other, pull_mine = (
        call(
            functools.partial(pull_kernel, first),
            vec,
            [WHOLE, WHOLE],
            12,
            (nrhs * update_rows.size, 2 * update_rows.size),
        )(pulled, update_rows)
        for first in (half, 0)
    )
    pull_mine = pull_mine + swap(pull_other, "col", cols, 1)
    pull_mine, pull_other = sum_over_lines(pull_mine, cols)
    share = leaf_cols // rows
    if inside and share % BLOCK == 0:
        def parts_of(masks):
            halves = [
                call(
                    functools.partial(solve_parts_kernel, rows, masks, first),
                    (jax.ShapeDtypeStruct((nrhs, half * share + (0 if first else sep_rows)), F32),)
                    * len(masks),
                    [WHOLE] * 4,
                    16,
                    (leaf_flops * len(masks) // (2 * rows), 2 * leaf_inverse.size * len(masks) // rows),
                )(vectors, pull, own, leaf_inverse)
                for first, vectors, pull in ((0, mine, pull_mine), (half, other, pull_other))
            ]
            return [jnp.concatenate(pair, 1) for pair in zip(*halves, strict=True)]

        far_parts = [swap(part, "row", rows, k) for k, part in enumerate(parts_of(tuple(range(1, rows))), 1)]
        parts = parts_of((0,)) + far_parts
        return call(
            finish_kernel,
            (
                jax.ShapeDtypeStruct((subs, nrhs, share), F32),
                jax.ShapeDtypeStruct((nrhs, sep_rows), F32),
            ),
            [WHOLE] * rows,
            4,
            (parts[0].size * rows, 4 * parts[0].size * rows),
        )(*parts)
    terms = call(
        solve_kernel,
        jax.ShapeDtypeStruct((subs, nrhs, leaf_cols), F32),
        [WHOLE] * 5,
        16,
        (leaf_flops, 4 * leaf_inverse.size),
    )(mine, other, pull_mine, pull_other, leaf_inverse)

    def last(k):
        leaf_part = lax.dynamic_slice_in_dim(terms, (row ^ k) * share, share, 2)
        own_part = lax.dynamic_slice_in_dim(own, (row ^ k) * sep_rows, sep_rows, 1)
        return jnp.concatenate([*leaf_part, own_part], 1)

    parts = [last(0)] + [swap(last(k), "row", rows, k) for k in range(1, rows)]
    done = sum(parts[1:]) + parts[0]
    leaf_solution = jnp.stack([done[:, s * share : (s + 1) * share] for s in range(subs)])
    return (leaf_solution, done[:, subs * share :])


def solution(mesh):
    sizes = tuple(mesh.shape[a] for a in ("leaf", "row", "col"))
    in_specs = (
        P("leaf", None, "col"),
        P("leaf", "row", "col"),
        P("leaf", "col", "row"),
        P("leaf", None),
        P(),
        P(("leaf", "row", "col"), None),
    )
    out_specs = (P("leaf", None, ("col", "row")), P(None, ("leaf", "row", "col")))
    return jax.shard_map(
        functools.partial(body, sizes), mesh=mesh, in_specs=in_specs, out_specs=out_specs, check_vma=False
    )
```
